512 devices in a mesh: outer: 4 (over x), dp: 128 (over z, y, core).
Axes of the slice: x: 4, y: 8, z: 8, core: 2. Of those that a mesh axis runs over, the one named last changes fastest.
Arguments:
- feats: bfloat16 [65536, 3072], P(('outer', 'dp')), may hold values from -24 to 24
- ln_gain: float32 [2048], replicated, may hold values from 0.5 to 1.5
- ln_bias: float32 [2048], replicated, may hold values from -3 to 3
- head_weight: bfloat16 [2048, 512], P('dp'), may hold values from -0.125 to 0.125
- captions: bfloat16 [262144, 512], P(('outer', 'dp'))
- image_cluster: int32 [65536], P(('outer', 'dp')), may hold values from 0 to 511, as said below
- image_target: int32 [65536], P(('outer', 'dp')), may hold values from 0 to 127, as said below
- cluster_owner: int32 [4, 512], P('outer'), may hold values from 0 to 127, as said below
- cluster_size: int32 [4, 512], P('outer'), may hold values from 1 to 128, as said below
- cap_index: int32 [4, 512, 128], P('outer'), may hold values from 0 to 511, as said below
- cotangent: float32 [65536], P(('outer', 'dp')), may hold values from -8 to 8
Outputs:
- feat_grad: bfloat16 [65536, 3072], P(('outer', 'dp'))
- weight_grad: float32 [2048, 512], P('dp')
- gain_grad: float32 [2048], replicated
- bias_grad: float32 [2048], replicated
The draws below stay inside these ranges and needn't reach their ends.
Inputs may be any that keep to these rules, and one draw needn't show every extreme that they name: `cluster_owner`: each dp index of a replica owns exactly 4 of its clusters. `cluster_size`: every replica has a cluster of 128 captions. `cap_index`: the first cluster_size entries of a cluster's row are distinct; the entries after them are not read. `image_cluster`: the images of one device belong to clusters of at most 2 images per owner; in each replica one owner receives exactly 2 images from every device. `image_target`: less than the size of the image's cluster.
All inputs are finite; a program needn't handle non-finite values.
Results may differ from the reference program's by a relative error of at most 0.012.
The reference program's roundings to bfloat16 on the way count: a program that leaves them out, or rounds other values in their place, can miss the bound.
Values may be sent and summed in bfloat16 or wider, within the bound.
No kernel may reach another device: no remote copies, remote signals or barrier semaphores. Data moves between devices by JAX's collectives and lax.ppermute only.
A program may use at most 64 MiB of HBM per device.

```python
import jax
import jax.numpy as jnp
from jax import lax

F = 3072
W_IN = 2048
E = 512
IMG_DEV = 128
CAP_DEV = 512
CL_DEV = 4
KMAX = 128
CAPACITY = 2
IMAGES = 65536
CAPTIONS = 262144
N_OUTER = 4
N_DP = 128


def cluster_plan(key):
    key_owner, key_first, key_second, key_busy, key_slots, key_captions, key_shuffle, key_local = jax.random.split(key, 8)
    count = CL_DEV * N_DP
    perms = jax.vmap(lambda piece: jax.random.permutation(piece, count))(jax.random.split(key_owner, N_OUTER))
    owners = (perms // CL_DEV).astype(jnp.int32)
    inverse = jnp.argsort(perms, axis=1, stable=True).astype(jnp.int32)
    first_draw = jax.random.randint(key_first, (N_OUTER, count), 1, KMAX + 1)
    second_draw = jax.random.randint(key_second, (N_OUTER, count), 1, KMAX + 1)
    cluster_sizes = jnp.minimum(first_draw, second_draw).at[:, 0].set(KMAX).astype(jnp.int32)
    busiest = jax.random.randint(key_busy, (N_OUTER,), 0, N_DP)
    slot_count = N_DP * CAPACITY
    slot_perm = jax.vmap(lambda piece: jax.random.permutation(piece, slot_count))(jax.random.split(key_slots, N_OUTER * N_DP)).reshape(N_OUTER, N_DP, slot_count)
    elsewhere = (slot_perm // CAPACITY != busiest[:, None, None]).astype(jnp.int32)
    ordering = jnp.argsort(elsewhere, axis=2, stable=True)
    ordered = jnp.take_along_axis(slot_perm, ordering, axis=2)[:, :, :IMG_DEV]
    shuffled = jax.vmap(lambda piece: jax.random.permutation(piece, IMG_DEV))(jax.random.split(key_shuffle, N_OUTER * N_DP)).reshape(N_OUTER, N_DP, IMG_DEV)
    image_owner = jnp.take_along_axis(ordered, shuffled, axis=2) // CAPACITY
    local_pick = jax.random.randint(key_local, (N_OUTER, N_DP, IMG_DEV), 0, CL_DEV)
    clusters = jax.vmap(lambda table, where_at: table[where_at])(inverse, image_owner * CL_DEV + local_pick)
    image_sizes = jax.vmap(lambda table, where_at: table[where_at])(cluster_sizes, clusters)
    targets = jax.random.randint(jax.random.fold_in(key_local, 5), (N_OUTER, N_DP, IMG_DEV), 0, 1 << 20) % image_sizes
    cap_perm = jax.vmap(lambda piece: jax.random.permutation(piece, CAP_DEV))(jax.random.split(key_captions, N_OUTER * count))
    cap_rows = cap_perm[:, :KMAX].reshape(N_OUTER, count, KMAX).astype(jnp.int32)
    return (owners, cluster_sizes, clusters.reshape(-1).astype(jnp.int32), targets.reshape(-1).astype(jnp.int32), cap_rows)


def draw_image_cluster(key, part):
    return cluster_plan(key)[2]


def draw_image_target(key, part):
    return cluster_plan(key)[3]


def draw_cluster_owner(key, part):
    return cluster_plan(key)[0]


def draw_cluster_size(key, part):
    return cluster_plan(key)[1]


def draw_cap_index(key, part):
    return cluster_plan(key)[4]


def draw_captions(key, part):
    key = jax.random.fold_in(key, 11)
    key_base = jax.random.fold_in(key, 0)
    base = jax.random.normal(key_base, (CAPTIONS, E), jnp.float32) / jnp.sqrt(jnp.float32(E))
    return base.astype(jnp.bfloat16)


def strengthened(entries, stream_key, source, target, parts, factor):
    def block_of(position):
        return (jnp.arange(entries.shape[position]) // (entries.shape[position] // parts)).reshape((-1,) + (1,) * (entries.ndim - 1 - position))

    one_side = jax.random.permutation(stream_key, parts)[block_of(target)]
    far = (block_of(target) + parts // 2) % parts
    return jnp.where((block_of(source) == one_side) | (block_of(source) == far), factor * entries, entries)


def levels(stream_key, dims, shards, low, largest):
    gain, own = 1.0, jax.random.fold_in(stream_key, 6)
    for position, shards_of in shards:
        heights = jnp.exp(jax.random.uniform(jax.random.fold_in(own, position), (shards_of,), jnp.float32, low / len(shards), largest / len(shards)))
        gain = gain * jnp.repeat(heights, dims[position] // shards_of).reshape([-1 if axis == position else 1 for axis in range(len(dims))])
    return gain


def bell_draw(rng, shape, spread, limit, cuts=(), kind=jnp.bfloat16):
    entries = spread * jax.random.normal(rng, shape, jnp.float32)
    if cuts:
        entries = entries * levels(rng, shape, cuts, -0.22, 0.18)
    return jnp.clip(entries, -limit, limit).astype(kind)


def heavy_noise(stream_key, shape, width, reach, cuts, heavy, kind=jnp.bfloat16):
    array = width * jax.random.normal(stream_key, shape, jnp.float32)
    if cuts:
        array = array * levels(stream_key, shape, cuts, -0.22, 0.18)
    return jnp.clip(strengthened(array, jax.random.fold_in(stream_key, 3), *heavy), -reach, reach).astype(kind)


def setup_inputs(seed: int = 0) -> dict:
    streams_of = jax.random.split(jax.random.key(seed), 12)
    return {
        "feats": heavy_noise(streams_of[0], (IMAGES, F), 1.0, 24.0, ((0, 512),), (0, 1, 512, 6.0)),
        "ln_gain": jnp.clip(1.0 + 0.1 * jax.random.normal(streams_of[1], (W_IN,), jnp.float32), 0.5, 1.5),
        "ln_bias": bell_draw(streams_of[2], (W_IN,), 0.5, 3.0, (), jnp.float32),
        "head_weight": bell_draw(streams_of[3], (W_IN, E), W_IN ** -0.5, 0.125, ((0, 128),)),
        "captions": draw_captions(jax.random.fold_in(streams_of[11], 71), 0),
        "image_cluster": draw_image_cluster(jax.random.fold_in(streams_of[11], 71), 0),
        "image_target": draw_image_target(jax.random.fold_in(streams_of[11], 71), 0),
        "cluster_owner": draw_cluster_owner(jax.random.fold_in(streams_of[11], 71), 0),
        "cluster_size": draw_cluster_size(jax.random.fold_in(streams_of[11], 71), 0),
        "cap_index": draw_cap_index(jax.random.fold_in(streams_of[11], 71), 0),
        "cotangent": bell_draw(streams_of[10], (IMAGES,), 2.0, 8.0, ((0, 512),), jnp.float32),
    }


logit_scale = 100.0

def reference(feats, ln_gain, ln_bias, head_weight, captions, image_cluster, image_target, cluster_owner, cluster_size, cap_index, cotangent):
    blocks = IMAGES // IMG_DEV
    feat_blocks = feats.reshape(blocks, IMG_DEV, F)
    cluster_blocks = image_cluster.reshape(blocks, IMG_DEV)
    target_blocks = image_target.reshape(blocks, IMG_DEV)
    cot_blocks = cotangent.reshape(blocks, IMG_DEV)
    indices = jnp.arange(blocks, dtype=jnp.int32)
    columns = jnp.arange(KMAX, dtype=jnp.int32)[None, :]

    def step(carry, inputs):
        weight_sum, gain_sum, bias_sum = carry
        block_feats, block_cluster, block_target, block_cot, device = inputs
        replica = device // N_DP
        widened = block_feats.astype(jnp.float32)
        means = lax.optimization_barrier(jnp.mean(widened, axis=1, keepdims=True))
        centred = widened - means
        inv_std = lax.rsqrt(lax.optimization_barrier(jnp.mean(centred * centred, axis=1, keepdims=True)) + 1e-05)
        normed = centred * inv_std
        window_bf = (normed[:, :W_IN] * ln_gain + ln_bias).astype(jnp.bfloat16)
        projected = jnp.dot(window_bf, head_weight, preferred_element_type=jnp.float32)
        norm_len = jnp.sqrt(lax.optimization_barrier(jnp.sum(projected * projected, axis=1, keepdims=True)) + 1e-06)
        unit = projected / norm_len
        unit_bf = unit.astype(jnp.bfloat16)
        owners = cluster_owner[replica][block_cluster]
        lengths = cluster_size[replica][block_cluster]
        selected = cap_index[replica][block_cluster]
        caption_rows = ((replica * N_DP + owners) * CAP_DEV).astype(jnp.int32)[:, None] + selected
        gathered = captions[caption_rows].astype(jnp.float32)
        scores = logit_scale * jnp.einsum('ie,ike->ik', unit_bf.astype(jnp.float32), gathered)
        valid = columns < lengths[:, None]
        highest = lax.optimization_barrier(jnp.max(jnp.where(valid, scores, -jnp.inf), axis=1, keepdims=True))
        weights = jnp.where(valid, jnp.exp(scores - highest), 0.0)
        probs = weights / lax.optimization_barrier(jnp.sum(weights, axis=1, keepdims=True))
        positive = (columns == block_target[:, None]).astype(jnp.float32)
        coefficients = (logit_scale * (probs - positive)).astype(jnp.bfloat16)
        unit_grad0 = jnp.einsum('ik,ike->ie', coefficients.astype(jnp.float32), gathered).astype(jnp.bfloat16)
        unit_grad = block_cot[:, None] * unit_grad0.astype(jnp.float32)
        proj_grad = (unit_grad - unit * lax.optimization_barrier(jnp.sum(unit * unit_grad, axis=1, keepdims=True))) / norm_len
        proj_bf = proj_grad.astype(jnp.bfloat16)
        weight_sum = weight_sum + jnp.dot(window_bf.T, proj_bf, preferred_element_type=jnp.float32)
        window_grad = jnp.dot(proj_bf, head_weight.T, preferred_element_type=jnp.float32)
        gain_sum = gain_sum + lax.optimization_barrier(jnp.sum(window_grad * normed[:, :W_IN], axis=0))
        bias_sum = bias_sum + lax.optimization_barrier(jnp.sum(window_grad, axis=0))
        normed_grad = jnp.concatenate([window_grad * ln_gain, jnp.zeros((IMG_DEV, F - W_IN), jnp.float32)], axis=1)
        feat_grad = inv_std * (normed_grad - lax.optimization_barrier(jnp.mean(normed_grad, axis=1, keepdims=True)) - normed * lax.optimization_barrier(jnp.mean(normed_grad * normed, axis=1, keepdims=True)))
        return ((weight_sum, gain_sum, bias_sum), feat_grad.astype(jnp.bfloat16))
    start = (jnp.zeros((W_IN, E), jnp.float32), jnp.zeros((W_IN,), jnp.float32), jnp.zeros((W_IN,), jnp.float32))
    sums, grads = lax.scan(step, start, (feat_blocks, cluster_blocks, target_blocks, cot_blocks, indices))
    return (grads.reshape(IMAGES, F), sums[0], sums[1], sums[2])
```

```python
import jax
import jax.numpy as jnp
from jax import lax
from jax.sharding import Mesh, PartitionSpec as P

logit_scale = 100.0
bf16 = jnp.bfloat16
f32 = jnp.float32
DP = ("z", "y", "core")
ALL = ("outer", "z", "y", "core")


def split_sum(value):
    high = lax.reduce_precision(value, 8, 7)
    return jnp.concatenate([high.astype(bf16), (value - high).astype(bf16)], axis=0)


def swap(value, axis, flip):
    size = lax.axis_size(axis)
    return lax.ppermute(value, axis, [(i, i ^ flip) for i in range(size)])


def owner_tables(captions, owner_table, size_table, index_table, me):
    count = owner_table.shape[0]
    kmax = index_table.shape[1]
    held = 4
    mine = (owner_table == me).astype(jnp.int32)
    ids = jnp.arange(count, dtype=jnp.int32)
    before = jnp.sum(jnp.where(ids[None, :] < ids[:, None], mine[None, :], 0), axis=1)
    chosen = (mine[None, :] > 0) & (before[None, :] == jnp.arange(held, dtype=jnp.int32)[:, None])
    picked = jnp.sum(jnp.where(chosen, ids[None, :], 0), axis=1)
    lengths = jnp.sum(jnp.where(chosen, size_table[None, :], 0), axis=1)
    rows = index_table.at[picked].get(mode="promise_in_bounds")
    used = (jnp.arange(kmax, dtype=jnp.int32)[None, :] < lengths[:, None]).reshape(1, held * kmax)
    place = rows.reshape(held * kmax, 1) == jnp.arange(captions.shape[0], dtype=jnp.int32)[None, :]
    ordered = jnp.dot(place.astype(bf16), captions, preferred_element_type=f32).astype(bf16)
    return ordered, used


def owner_work(rows, ordered, used, kmax):
    width = ordered.shape[1]
    embedded = rows[:, :width]
    local = rows[:, width : width + 1].astype(f32)
    target = rows[:, width + 1 : width + 2].astype(f32)
    columns = jnp.arange(ordered.shape[0], dtype=jnp.int32)[None, :]
    cluster_of = (columns // kmax).astype(f32)
    scores = logit_scale * lax.dot_general(
        embedded, ordered, (((1,), (1,)), ((), ())), preferred_element_type=f32
    )
    valid = used & (cluster_of == local)
    highest = jnp.max(jnp.where(valid, scores, -jnp.inf), axis=1, keepdims=True)
    weights = jnp.where(valid, jnp.exp(scores - highest), 0.0)
    probs = weights / jnp.sum(weights, axis=1, keepdims=True)
    positive = (columns.astype(f32) == local * kmax + target).astype(f32)
    coefficients = (logit_scale * (probs - positive)).astype(bf16)
    return jnp.dot(coefficients, ordered, preferred_element_type=f32).astype(bf16)


def body(
    feats,
    ln_gain,
    ln_bias,
    head_weight,
    captions,
    image_cluster,
    image_target,
    cluster_owner,
    cluster_size,
    cap_index,
    cotangent,
):
    count, width = feats.shape
    window_width = ln_gain.shape[0]
    embed_width = head_weight.shape[1]
    shard = head_weight.shape[0]
    nz, ny, nc = lax.axis_size("z"), lax.axis_size("y"), lax.axis_size("core")
    dp_count = nz * ny * nc
    half = window_width // nc
    core = lax.axis_index("core")
    me = lax.axis_index(DP)
    capacity = 2
    kmax = cap_index.shape[2]
    owner_table = cluster_owner[0]

    weight_z = lax.all_gather(head_weight, "z", axis=0, tiled=True)
    weight_own = lax.all_gather(weight_z, "y", axis=0, tiled=True)
    weight_other = swap(weight_own, "core", 1)

    widened = feats.astype(f32)
    means = jnp.mean(widened, axis=1, keepdims=True)
    centred = widened - means
    inv_std = lax.rsqrt(jnp.mean(centred * centred, axis=1, keepdims=True) + 1e-05)
    normed_head = centred[:, :window_width] * inv_std
    normed_tail = centred[:, window_width:] * inv_std
    window_bf = (normed_head * ln_gain + ln_bias).astype(bf16)
    by_feature = (
        window_bf.T.reshape(nz, ny, nc, shard, count).transpose(2, 1, 0, 3, 4).reshape(nc, half, count)
    )
    window_own = lax.dynamic_index_in_dim(by_feature, core, 0, keepdims=False)
    window_other = lax.dynamic_index_in_dim(by_feature, 1 - core, 0, keepdims=False)

    ids = jnp.arange(owner_table.shape[0], dtype=jnp.int32)[None, :]
    owners = jnp.sum(jnp.where(image_cluster[:, None] == ids, owner_table[None, :], 0), axis=1)
    local = jnp.sum(
        ((owner_table[None, :] == owners[:, None]) & (ids < image_cluster[:, None])).astype(jnp.int32), axis=1
    )
    images = jnp.arange(count, dtype=jnp.int32)
    ranks = jnp.sum(
        ((owners[:, None] == owners[None, :]) & (images[None, :] < images[:, None])).astype(jnp.int32), axis=1
    )
    slots = owners * capacity + ranks
    place = (jnp.arange(dp_count * capacity, dtype=jnp.int32)[:, None] == slots[None, :]).astype(bf16)
    labels = jnp.stack([local, image_target], axis=1).astype(bf16)
    labels = jnp.concatenate([labels, jnp.zeros((count, 126), bf16)], axis=1)
    ordered, used = owner_tables(captions, owner_table, cluster_size[0], cap_index[0], me)

    def by_rows(left, right):
        return lax.dot_general(left, right, (((0,), (0,)), ((), ())), preferred_element_type=f32)

    projected = by_rows(window_own, weight_own) + by_rows(window_other, weight_other)
    norm_len = jnp.sqrt(jnp.sum(projected * projected, axis=1, keepdims=True) + 1e-06)
    unit = projected / norm_len
    payload = jnp.concatenate([unit.astype(bf16), labels], axis=1)
    send_rows = jnp.dot(place, payload, preferred_element_type=f32).astype(bf16)
    received = lax.all_to_all(
        send_rows.reshape(dp_count, capacity, -1), DP, split_axis=0, concat_axis=0, tiled=True
    )
    gradient = owner_work(received.reshape(dp_count * capacity, -1), ordered, used, kmax)
    returned = lax.all_to_all(
        gradient.reshape(dp_count, capacity, embed_width), DP, split_axis=0, concat_axis=0, tiled=True
    )
    unit_grad0 = by_rows(place, returned.reshape(dp_count * capacity, embed_width))
    unit_grad = cotangent[:, None] * unit_grad0
    proj_grad = (unit_grad - unit * jnp.sum(unit * unit_grad, axis=1, keepdims=True)) / norm_len
    proj_bf = proj_grad.astype(bf16)

    term_other = jnp.dot(window_other, proj_bf, preferred_element_type=f32).astype(bf16)
    term = jnp.dot(window_own, proj_bf, preferred_element_type=f32) + swap(term_other, "core", 1).astype(f32)

    first = jnp.where(core == 0, weight_own, weight_other)
    second = jnp.where(core == 0, weight_other, weight_own)
    full_weight = (
        jnp.stack([first, second])
        .reshape(nc, ny, nz, shard, embed_width)
        .transpose(2, 1, 0, 3, 4)
        .reshape(window_width, embed_width)
    )
    window_grad = lax.dot_general(
        proj_bf, full_weight, (((1,), (1,)), ((), ())), preferred_element_type=f32
    )
    gain_local = jnp.sum(window_grad * normed_head, axis=0)
    bias_local = jnp.sum(window_grad, axis=0)
    sums = jnp.concatenate([gain_local, bias_local]).reshape(-1, embed_width)
    depth = sums.shape[0]
    sums = sums + swap(sums, "core", 1)

    for axis, parts in (("y", ny), ("z", nz)):
        both = split_sum(sums)
        pieces = jnp.concatenate(
            [
                term.astype(bf16).reshape(parts, -1, embed_width),
                jnp.broadcast_to(both[None], (parts,) + both.shape),
            ],
            axis=1,
        )
        pieces = lax.all_to_all(pieces, axis, split_axis=0, concat_axis=0, tiled=True)
        total = jnp.sum(pieces.astype(f32), axis=0)
        term = total[: -2 * depth]
        sums = total[-2 * depth : -depth] + total[-depth:]

    both = jnp.concatenate([term, sums], axis=0)
    both = (both + swap(both, "outer", 2)) + (swap(both, "outer", 1) + swap(both, "outer", 3))
    weight_grad = both[:shard]
    gain_grad = both[shard : shard + depth // 2].reshape(window_width)
    bias_grad = both[shard + depth // 2 :].reshape(window_width)

    scaled_grad = window_grad * ln_gain
    first_mean = jnp.sum(scaled_grad, axis=1, keepdims=True) / width
    second_mean = jnp.sum(scaled_grad * normed_head, axis=1, keepdims=True) / width
    grad_head = inv_std * (scaled_grad - first_mean - normed_head * second_mean)
    grad_tail = inv_std * (0.0 - first_mean - normed_tail * second_mean)
    feat_grad = jnp.concatenate([grad_head.astype(bf16), grad_tail.astype(bf16)], axis=1)
    return (feat_grad, weight_grad, gain_grad, bias_grad)


def solution(mesh):
    outer, dp = mesh.devices.shape
    fine = Mesh(mesh.devices.reshape(outer, 8, dp // 16, 2), ALL)
    in_specs = (
        P(ALL, None),
        P(),
        P(),
        P(DP, None),
        P(ALL, None),
        P(ALL),
        P(ALL),
        P("outer", None),
        P("outer", None),
        P("outer", None, None),
        P(ALL),
    )
    out_specs = (P(ALL, None), P(DP, None), P(), P())
    return jax.shard_map(body, mesh=fine, in_specs=in_specs, out_specs=out_specs, check_vma=False)
```

```python
import jax
import jax.numpy as jnp
from jax import lax
from jax.sharding import Mesh, PartitionSpec as P

logit_scale = 100.0
bf16 = jnp.bfloat16
f32 = jnp.float32
DP = ("z", "y", "core")
ALL = ("outer", "z", "y", "core")


def swap(value, axis, flip):
    size = lax.axis_size(axis)
    return lax.ppermute(value, axis, [(i, i ^ flip) for i in range(size)])


def split_sum(value, axis):
    high = lax.reduce_precision(value, 8, 7)
    return jnp.concatenate([high.astype(bf16), (value - high).astype(bf16)], axis=axis)


def exchange(pieces, axis):
    return lax.all_to_all(pieces, axis, split_axis=0, concat_axis=0, tiled=True)


def gather(value, axis):
    size = lax.axis_size(axis)
    return exchange(jnp.broadcast_to(value[None], (size,) + value.shape), axis)


def side_by_side(blocks):
    return jnp.concatenate([blocks[i] for i in range(blocks.shape[0])], axis=1)


def owner_tables(captions, owner_table, size_table, index_table, me):
    count = owner_table.shape[0]
    kmax = index_table.shape[1]
    held = 4
    mine = (owner_table == me).astype(jnp.int32)
    ids = jnp.arange(count, dtype=jnp.int32)
    before = jnp.sum(jnp.where(ids[None, :] < ids[:, None], mine[None, :], 0), axis=1)
    chosen = (mine[None, :] > 0) & (before[None, :] == jnp.arange(held, dtype=jnp.int32)[:, None])
    picked = jnp.sum(jnp.where(chosen, ids[None, :], 0), axis=1)
    lengths = jnp.sum(jnp.where(chosen, size_table[None, :], 0), axis=1)
    rows = index_table.at[picked].get(mode="promise_in_bounds")
    used = (jnp.arange(kmax, dtype=jnp.int32)[None, :] < lengths[:, None]).reshape(1, held * kmax)
    place = rows.reshape(held * kmax, 1) == jnp.arange(captions.shape[0], dtype=jnp.int32)[None, :]
    ordered = jnp.dot(place.astype(bf16), captions, preferred_element_type=f32).astype(bf16)
    return ordered, used


def owner_work(rows, ordered, used, kmax):
    width = ordered.shape[1]
    embedded = rows[:, :width]
    local = rows[:, width : width + 1].astype(f32)
    target = rows[:, width + 1 : width + 2].astype(f32)
    columns = jnp.arange(ordered.shape[0], dtype=jnp.int32)[None, :]
    cluster_of = (columns // kmax).astype(f32)
    scores = logit_scale * lax.dot_general(
        embedded, ordered, (((1,), (1,)), ((), ())), preferred_element_type=f32
    )
    valid = used & (cluster_of == local)
    highest = jnp.max(jnp.where(valid, scores, -jnp.inf), axis=1, keepdims=True)
    weights = jnp.where(valid, jnp.exp(scores - highest), 0.0)
    probs = weights / jnp.sum(weights, axis=1, keepdims=True)
    positive = (columns.astype(f32) == local * kmax + target).astype(f32)
    coefficients = (logit_scale * (probs - positive)).astype(bf16)
    return jnp.dot(coefficients, ordered, preferred_element_type=f32).astype(bf16)


def body(
    feats,
    ln_gain,
    ln_bias,
    head_weight,
    captions,
    image_cluster,
    image_target,
    cluster_owner,
    cluster_size,
    cap_index,
    cotangent,
):
    count, width = feats.shape
    window_width = ln_gain.shape[0]
    embed_width = head_weight.shape[1]
    shard = head_weight.shape[0]
    nz, ny, nc = lax.axis_size("z"), lax.axis_size("y"), lax.axis_size("core")
    dp_count = nz * ny * nc
    half = window_width // nc
    core = lax.axis_index("core")
    me = lax.axis_index(DP)
    capacity = 2
    kmax = cap_index.shape[2]
    owner_table = cluster_owner[0]

    outer = lax.axis_index("outer")
    n_outer = lax.axis_size("outer")
    block = embed_width // n_outer
    columns = lax.dynamic_slice_in_dim(head_weight, outer * block, block, 1)
    columns = gather(columns, ("z", "y")).reshape(half, block)
    weight_own = side_by_side(gather(columns, "outer"))

    widened = feats.astype(f32)
    means = jnp.mean(widened, axis=1, keepdims=True)
    centred = widened - means
    inv_std = lax.rsqrt(jnp.mean(centred * centred, axis=1, keepdims=True) + 1e-05)
    normed_head = centred[:, :window_width] * inv_std
    normed_tail = centred[:, window_width:] * inv_std
    window_bf = (normed_head * ln_gain + ln_bias).astype(bf16)
    by_feature = window_bf.T.reshape(nz * ny, nc, shard, count)
    window_own = lax.dynamic_index_in_dim(by_feature, core, 1, keepdims=False).reshape(half, count)
    window_other = lax.dynamic_index_in_dim(by_feature, 1 - core, 1, keepdims=False).reshape(half, count)
    window_sent = swap(window_other, "core", 1)
    window_pair = jnp.concatenate(
        [jnp.where(core == 0, window_own, window_sent), jnp.where(core == 0, window_sent, window_own)], axis=1
    )
    window_all = side_by_side(lax.all_gather(window_pair, "outer", axis=0))

    ids = jnp.arange(owner_table.shape[0], dtype=jnp.int32)[None, :]
    owners = jnp.sum(jnp.where(image_cluster[:, None] == ids, owner_table[None, :], 0), axis=1)
    local = jnp.sum(
        ((owner_table[None, :] == owners[:, None]) & (ids < image_cluster[:, None])).astype(jnp.int32), axis=1
    )
    images = jnp.arange(count, dtype=jnp.int32)
    ranks = jnp.sum(
        ((owners[:, None] == owners[None, :]) & (images[None, :] < images[:, None])).astype(jnp.int32), axis=1
    )
    slots = owners * capacity + ranks
    place = (jnp.arange(dp_count * capacity, dtype=jnp.int32)[:, None] == slots[None, :]).astype(bf16)
    labels = jnp.stack([local, image_target], axis=1).astype(bf16)
    labels = jnp.concatenate([labels, jnp.zeros((count, 126), bf16)], axis=1)
    ordered, used = owner_tables(captions, owner_table, cluster_size[0], cap_index[0], me)

    def by_rows(left, right):
        return lax.dot_general(left, right, (((0,), (0,)), ((), ())), preferred_element_type=f32)

    partial = by_rows(window_pair, weight_own).reshape(nc, count, embed_width)
    partial_own = lax.dynamic_index_in_dim(partial, core, 0, keepdims=False)
    partial_other = lax.dynamic_index_in_dim(partial, 1 - core, 0, keepdims=False)
    partial_sent = swap(partial_other, "core", 1)
    projected = partial_own + partial_sent
    weight_own, projected = lax.optimization_barrier((weight_own, projected))
    weight_other = swap(weight_own, "core", 1)
    first = jnp.where(core == 0, weight_own, weight_other).reshape(nz * ny, 1, shard, embed_width)
    second = jnp.where(core == 0, weight_other, weight_own).reshape(nz * ny, 1, shard, embed_width)
    full_weight = jnp.concatenate([first, second], axis=1).reshape(window_width, embed_width)
    norm_len = jnp.sqrt(jnp.sum(projected * projected, axis=1, keepdims=True) + 1e-06)
    unit = projected / norm_len
    payload = jnp.concatenate([unit.astype(bf16), labels], axis=1)
    send_rows = jnp.dot(place, payload, preferred_element_type=f32).astype(bf16)
    received = lax.all_to_all(
        send_rows.reshape(dp_count, capacity, -1), DP, split_axis=0, concat_axis=0, tiled=True
    )
    gradient = owner_work(received.reshape(dp_count * capacity, -1), ordered, used, kmax)
    window_all, gradient = lax.optimization_barrier((window_all, gradient))
    returned = lax.all_to_all(
        gradient.reshape(dp_count, capacity, embed_width), DP, split_axis=0, concat_axis=0, tiled=True
    )
    unit_grad0 = by_rows(place, returned.reshape(dp_count * capacity, embed_width))
    unit_grad = cotangent[:, None] * unit_grad0
    proj_grad = (unit_grad - unit * jnp.sum(unit * unit_grad, axis=1, keepdims=True)) / norm_len
    proj_bf = proj_grad.astype(bf16)

    window_grad = lax.dot_general(
        proj_bf, full_weight, (((1,), (1,)), ((), ())), preferred_element_type=f32
    )
    gain_local = jnp.sum(window_grad * normed_head, axis=0)
    bias_local = jnp.sum(window_grad, axis=0)

    group = n_outer * nc
    sums = jnp.concatenate([gain_local, bias_local]).reshape(group, -1, block)
    depth = sums.shape[1]
    blocks = jnp.concatenate([proj_bf[:, i * block : (i + 1) * block] for i in range(n_outer)], axis=0)
    blocks = blocks.reshape(n_outer, 1, count, block)
    blocks = jnp.broadcast_to(blocks, (n_outer, nc, count, block)).reshape(group, count, block)
    pieces = exchange(jnp.concatenate([blocks, split_sum(sums, 1)], axis=1), ("outer", "core"))
    proj_all = pieces[:, :count].reshape(-1, block)
    sums = jnp.sum(pieces[:, count:].astype(f32), axis=0)
    sums = sums[:depth] + sums[depth:]

    term = jnp.dot(window_all, proj_all, preferred_element_type=f32).astype(bf16)
    sums = split_sum(sums, 0)
    sums = jnp.broadcast_to(sums[None], (nz * ny,) + sums.shape)
    pieces = exchange(jnp.concatenate([term.reshape(nz * ny, shard, block), sums], axis=1), ("z", "y"))
    pieces = jnp.sum(pieces.astype(f32), axis=0)
    sums = pieces[shard : shard + depth] + pieces[shard + depth :]

    last = gather(jnp.concatenate([pieces[:shard], sums], axis=0), ("outer", "core"))
    last = last.reshape(n_outer, nc, shard + depth, block)
    weight_grad = side_by_side(lax.dynamic_index_in_dim(last[:, :, :shard], core, 1, keepdims=False))
    sums = last[:, :, shard:].reshape(2, window_width)
    gain_grad, bias_grad = sums[0], sums[1]

    scaled_grad = window_grad * ln_gain
    first_mean = jnp.sum(scaled_grad, axis=1, keepdims=True) / width
    second_mean = jnp.sum(scaled_grad * normed_head, axis=1, keepdims=True) / width
    grad_head = inv_std * (scaled_grad - first_mean - normed_head * second_mean)
    grad_tail = inv_std * (0.0 - first_mean - normed_tail * second_mean)
    feat_grad = jnp.concatenate([grad_head.astype(bf16), grad_tail.astype(bf16)], axis=1)
    return (feat_grad, weight_grad, gain_grad, bias_grad)


def solution(mesh):
    outer, dp = mesh.devices.shape
    fine = Mesh(mesh.devices.reshape(outer, 8, dp // 16, 2), ALL)
    in_specs = (
        P(ALL, None),
        P(),
        P(),
        P(DP, None),
        P(ALL, None),
        P(ALL),
        P(ALL),
        P("outer", None),
        P("outer", None),
        P("outer", None, None),
        P(ALL),
    )
    out_specs = (P(ALL, None), P(DP, None), P(), P())
    return jax.shard_map(body, mesh=fine, in_specs=in_specs, out_specs=out_specs, check_vma=False)
```

```python
import functools

import jax
import jax.numpy as jnp
from jax import lax
from jax.experimental import pallas as pl
from jax.experimental.pallas import tpu as pltpu
from jax.sharding import Mesh, PartitionSpec as P

logit_scale = 100.0
bf16 = jnp.bfloat16
f32 = jnp.float32
DP = ("z", "y", "core")
ALL = ("outer", "z", "y", "core")


def swap(value, axis, flip):
    size = lax.axis_size(axis)
    return lax.ppermute(value, axis, [(i, i ^ flip) for i in range(size)])


def split_sum(value, axis):
    high = lax.reduce_precision(value, 8, 7)
    return jnp.concatenate([high.astype(bf16), (value - high).astype(bf16)], axis=axis)


def exchange(pieces, axis):
    return lax.all_to_all(pieces, axis, split_axis=0, concat_axis=0, tiled=True)


def gather(value, axis):
    size = lax.axis_size(axis)
    return exchange(jnp.broadcast_to(value[None], (size,) + value.shape), axis)


def side_by_side(blocks):
    return jnp.concatenate([blocks[i] for i in range(blocks.shape[0])], axis=1)


def owner_tables(captions, owner_table, size_table, index_table, me):
    count = owner_table.shape[0]
    kmax = index_table.shape[1]
    held = 4
    mine = (owner_table == me).astype(jnp.int32)
    ids = jnp.arange(count, dtype=jnp.int32)
    before = jnp.sum(jnp.where(ids[None, :] < ids[:, None], mine[None, :], 0), axis=1)
    chosen = (mine[None, :] > 0) & (before[None, :] == jnp.arange(held, dtype=jnp.int32)[:, None])
    picked = jnp.sum(jnp.where(chosen, ids[None, :], 0), axis=1)
    lengths = jnp.sum(jnp.where(chosen, size_table[None, :], 0), axis=1)
    rows = index_table.at[picked].get(mode="promise_in_bounds")
    used = (jnp.arange(kmax, dtype=jnp.int32)[None, :] < lengths[:, None]).reshape(1, held * kmax)
    place = rows.reshape(held * kmax, 1) == jnp.arange(captions.shape[0], dtype=jnp.int32)[None, :]
    ordered = jnp.dot(place.astype(bf16), captions, preferred_element_type=f32).astype(bf16)
    return ordered, used


def call(kernel, out_shape, *operands):
    return pl.pallas_call(
        kernel,
        out_shape=out_shape,
        compiler_params=pltpu.CompilerParams(vmem_limit_bytes=24 * 2**20),
    )(*operands)


def owner_kernel(kmax, parts, rows_ref, ordered_ref, used_ref, out_ref):
    count, (held, width) = rows_ref.shape[0], ordered_ref.shape
    block = width // parts
    ordered = ordered_ref[...]
    labels = rows_ref[:, width:].astype(f32).astype(jnp.int32)
    local, target = labels[:, 0:1], labels[:, 1:2]
    columns = lax.broadcasted_iota(jnp.int32, (count, held), 1)
    first = local * kmax
    valid = (used_ref[...] > 0) & (columns >= first) & (columns < first + kmax)
    scores = logit_scale * lax.dot_general(
        rows_ref[:, :width], ordered, (((1,), (1,)), ((), ())), preferred_element_type=f32
    )
    highest = jnp.max(jnp.where(valid, scores, -jnp.inf), axis=1, keepdims=True)
    weights = jnp.where(valid, jnp.exp(scores - highest), 0.0)
    probs = weights / jnp.sum(weights, axis=1, keepdims=True)
    positive = jnp.where(columns == first + target, 1.0, 0.0)
    coefficients = (logit_scale * (probs - positive)).astype(bf16)
    gradient = jnp.dot(coefficients, ordered, preferred_element_type=f32).astype(bf16)
    size = 16 * parts
    row = lax.broadcasted_iota(jnp.int32, (size, size), 0)
    column = lax.broadcasted_iota(jnp.int32, (size, size), 1)
    order = jnp.where(column == lax.rem(row, parts) * 16 + lax.div(row, parts), 1.0, 0.0).astype(bf16)
    for at in range(0, count, 16):
        some = jnp.concatenate([gradient[at : at + 16, i * block : (i + 1) * block] for i in range(parts)], axis=0)
        out_ref[at * parts : (at + 16) * parts, :] = jnp.dot(order, some, preferred_element_type=f32).astype(bf16)


def gradient_kernel(
    parts, depth, back_ref, slots_ref, unit_ref, norm_ref, cot_ref, weight_ref, normed_ref, pieces_ref, grad_ref
):
    group, rows, block = pieces_ref.shape
    count = unit_ref.shape[0]
    back, unit, slots = back_ref[...], unit_ref[...], slots_ref[...]
    columns = lax.broadcasted_iota(jnp.int32, (count, back.shape[0]), 1)
    blocks = []
    for i in range(parts):
        here = jnp.where(columns == slots * parts + i, 1.0, 0.0).astype(bf16)
        blocks.append(jnp.dot(here, back, preferred_element_type=f32))
    unit_grad = cot_ref[...] * jnp.concatenate(blocks, axis=1)
    along = jnp.sum(unit * unit_grad, axis=1, keepdims=True)
    proj = ((unit_grad - unit * along) / norm_ref[...]).astype(bf16)
    window_grad = lax.dot_general(
        proj, weight_ref[...], (((1,), (1,)), ((), ())), preferred_element_type=f32
    )
    grad_ref[...] = window_grad
    gain = jnp.sum(window_grad * normed_ref[...], axis=0, keepdims=True)
    bias = jnp.sum(window_grad, axis=0, keepdims=True)
    place = lax.broadcasted_iota(jnp.int32, (rows - count, block), 0)
    for g in range(group):
        tail = jnp.zeros((rows - count, block), f32)
        values, at = (gain, g) if g < group // 2 else (bias, g - group // 2)
        for r in range(depth):
            line = values[:, (at * depth + r) * block : (at * depth + r + 1) * block]
            high = line.astype(bf16).astype(f32)
            tail = jnp.where(place == r, high, jnp.where(place == depth + r, line - high, tail))
        i = g * parts // group
        pieces_ref[g, :count, :] = proj[:, i * block : (i + 1) * block]
        pieces_ref[g, count:, :] = tail.astype(bf16)


def term_kernel(windows_ref, pieces_ref, out_ref):
    groups, height, width = windows_ref.shape
    count = width // 2
    step = height // 4
    proj = [
        jnp.concatenate([pieces_ref[2 * g, :count, :], pieces_ref[2 * g + 1, :count, :]], axis=0)
        for g in range(groups)
    ]
    for at in range(0, height, step):
        total = jnp.dot(windows_ref[0, at : at + step, :], proj[0], preferred_element_type=f32)
        for g in range(1, groups):
            total += jnp.dot(windows_ref[g, at : at + step, :], proj[g], preferred_element_type=f32)
        out_ref[at : at + step, :] = total.astype(bf16)


def body(
    feats,
    ln_gain,
    ln_bias,
    head_weight,
    captions,
    image_cluster,
    image_target,
    cluster_owner,
    cluster_size,
    cap_index,
    cotangent,
):
    count, width = feats.shape
    window_width = ln_gain.shape[0]
    embed_width = head_weight.shape[1]
    shard = head_weight.shape[0]
    nz, ny, nc = lax.axis_size("z"), lax.axis_size("y"), lax.axis_size("core")
    dp_count = nz * ny * nc
    half = window_width // nc
    core = lax.axis_index("core")
    me = lax.axis_index(DP)
    capacity = 2
    kmax = cap_index.shape[2]
    owner_table = cluster_owner[0]

    outer = lax.axis_index("outer")
    n_outer = lax.axis_size("outer")
    block = embed_width // n_outer
    columns = lax.dynamic_slice_in_dim(head_weight, outer * block, block, 1)
    columns = gather(columns, ("z", "y")).reshape(half, block)
    blocks = [columns] + [swap(columns, "outer", i) for i in range(1, n_outer)]
    for bit in (1, 2):
        odd = (outer & bit) > 0
        blocks = [jnp.where(odd, blocks[i ^ bit], blocks[i]) for i in range(n_outer)]
    weight_own = jnp.concatenate(blocks, axis=1)


    widened = feats.astype(f32)
    means = jnp.mean(widened, axis=1, keepdims=True)
    centred = widened - means
    inv_std = lax.rsqrt(jnp.mean(centred * centred, axis=1, keepdims=True) + 1e-05)
    normed_head = centred[:, :window_width] * inv_std
    normed_tail = centred[:, window_width:] * inv_std
    window_bf = (normed_head * ln_gain + ln_bias).astype(bf16)
    by_feature = window_bf.T.reshape(nz * ny, nc, shard, count)
    window_own = lax.dynamic_index_in_dim(by_feature, core, 1, keepdims=False).reshape(half, count)
    window_other = lax.dynamic_index_in_dim(by_feature, 1 - core, 1, keepdims=False).reshape(half, count)
    window_sent = swap(window_other, "core", 1)
    window_pair = jnp.concatenate(
        [jnp.where(core == 0, window_own, window_sent), jnp.where(core == 0, window_sent, window_own)], axis=1
    )
    window_all = lax.all_gather(window_pair, "outer", axis=0)

    ids = jnp.arange(owner_table.shape[0], dtype=jnp.int32)[None, :]
    owners = jnp.sum(jnp.where(image_cluster[:, None] == ids, owner_table[None, :], 0), axis=1)
    local = jnp.sum(
        ((owner_table[None, :] == owners[:, None]) & (ids < image_cluster[:, None])).astype(jnp.int32), axis=1
    )
    images = jnp.arange(count, dtype=jnp.int32)
    ranks = jnp.sum(
        ((owners[:, None] == owners[None, :]) & (images[None, :] < images[:, None])).astype(jnp.int32), axis=1
    )
    slots = owners * capacity + ranks
    place = (jnp.arange(dp_count * capacity, dtype=jnp.int32)[:, None] == slots[None, :]).astype(bf16)
    labels = jnp.stack([local, image_target], axis=1).astype(bf16)
    labels = jnp.concatenate([labels, jnp.zeros((count, 126), bf16)], axis=1)
    ordered, used = owner_tables(captions, owner_table, cluster_size[0], cap_index[0], me)
    weight_own, ordered, used, place, labels = lax.optimization_barrier((weight_own, ordered, used, place, labels))

    def by_rows(left, right):
        return lax.dot_general(left, right, (((0,), (0,)), ((), ())), preferred_element_type=f32)

    partial = by_rows(window_pair, weight_own).reshape(nc, count, embed_width)
    partial_own = lax.dynamic_index_in_dim(partial, core, 0, keepdims=False)
    partial_other = lax.dynamic_index_in_dim(partial, 1 - core, 0, keepdims=False)
    partial_sent = swap(partial_other, "core", 1)
    projected = partial_own + partial_sent
    weight_own, projected = lax.optimization_barrier((weight_own, projected))
    weight_other = swap(weight_own, "core", 1)
    first = jnp.where(core == 0, weight_own, weight_other).reshape(nz * ny, 1, shard, embed_width)
    second = jnp.where(core == 0, weight_other, weight_own).reshape(nz * ny, 1, shard, embed_width)
    full_weight = jnp.concatenate([first, second], axis=1).reshape(window_width, embed_width)
    norm_len = jnp.sqrt(jnp.sum(projected * projected, axis=1, keepdims=True) + 1e-06)
    unit = projected / norm_len
    payload = jnp.concatenate([unit.astype(bf16), labels], axis=1)
    send_rows = jnp.dot(place, payload, preferred_element_type=f32).astype(bf16)
    received = lax.all_to_all(
        send_rows.reshape(dp_count, capacity, -1), DP, split_axis=0, concat_axis=0, tiled=True
    )
    gradient = call(
        functools.partial(owner_kernel, kmax, n_outer),
        jax.ShapeDtypeStruct((dp_count * capacity * n_outer, block), bf16),
        received.reshape(dp_count * capacity, -1),
        ordered,
        used.astype(f32),
    )
    window_all, gradient = lax.optimization_barrier((window_all, gradient))
    returned = exchange(gradient.reshape(dp_count, capacity * n_outer, block), DP).reshape(-1, block)

    group = n_outer * nc
    depth = 2 * window_width // (group * block)
    pieces, window_grad = call(
        functools.partial(gradient_kernel, n_outer, depth),
        (
            jax.ShapeDtypeStruct((group, count + 16, block), bf16),
            jax.ShapeDtypeStruct((count, window_width), f32),
        ),
        returned,
        slots[:, None],
        unit,
        norm_len,
        cotangent[:, None],
        full_weight,
        normed_head,
    )
    pieces = exchange(pieces, ("outer", "core"))
    sums = jnp.sum(pieces[:, count : count + 2 * depth].astype(f32), axis=0)
    sums = sums[:depth] + sums[depth:]

    term = call(term_kernel, jax.ShapeDtypeStruct((half, block), bf16), window_all, pieces)
    sums = split_sum(sums, 0)
    sums = jnp.broadcast_to(sums[None], (nz * ny,) + sums.shape)
    pieces = exchange(jnp.concatenate([term.reshape(nz * ny, shard, block), sums], axis=1), ("z", "y"))
    pieces = jnp.sum(pieces.astype(f32), axis=0)
    sums = pieces[shard : shard + depth] + pieces[shard + depth :]

    last = gather(jnp.concatenate([pieces[:shard], sums], axis=0), ("outer", "core"))
    last = last.reshape(n_outer, nc, shard + depth, block)
    weight_grad = side_by_side(lax.dynamic_index_in_dim(last[:, :, :shard], core, 1, keepdims=False))
    sums = last[:, :, shard:].reshape(2, window_width)
    gain_grad, bias_grad = sums[0], sums[1]

    scaled_grad = window_grad * ln_gain
    first_mean = jnp.sum(scaled_grad, axis=1, keepdims=True) / width
    second_mean = jnp.sum(scaled_grad * normed_head, axis=1, keepdims=True) / width
    grad_head = inv_std * (scaled_grad - first_mean - normed_head * second_mean)
    grad_tail = inv_std * (0.0 - first_mean - normed_tail * second_mean)
    feat_grad = jnp.concatenate([grad_head.astype(bf16), grad_tail.astype(bf16)], axis=1)
    return (feat_grad, weight_grad, gain_grad, bias_grad)


def solution(mesh):
    outer, dp = mesh.devices.shape
    fine = Mesh(mesh.devices.reshape(outer, 8, dp // 16, 2), ALL)
    in_specs = (
        P(ALL, None),
        P(),
        P(),
        P(DP, None),
        P(ALL, None),
        P(ALL),
        P(ALL),
        P("outer", None),
        P("outer", None),
        P("outer", None, None),
        P(ALL),
    )
    out_specs = (P(ALL, None), P(DP, None), P(), P())
    return jax.shard_map(body, mesh=fine, in_specs=in_specs, out_specs=out_specs, check_vma=False)
```

```python
import functools

import jax
import jax.numpy as jnp
from jax import lax
from jax.experimental import pallas as pl
from jax.experimental.pallas import tpu as pltpu
from jax.sharding import Mesh, PartitionSpec as P

logit_scale = 100.0
bf16 = jnp.bfloat16
f32 = jnp.float32
DP = ("z", "y", "core")
ALL = ("outer", "z", "y", "core")


def swap(value, axis, flip):
    size = lax.axis_size(axis)
    return lax.ppermute(value, axis, [(i, i ^ flip) for i in range(size)])


def split_sum(value, axis):
    high = lax.reduce_precision(value, 8, 7)
    return jnp.concatenate([high.astype(bf16), (value - high).astype(bf16)], axis=axis)


def exchange(pieces, axis):
    return lax.all_to_all(pieces, axis, split_axis=0, concat_axis=0, tiled=True)


def owner_tables(captions, owner_table, size_table, index_table, me):
    count = owner_table.shape[0]
    kmax = index_table.shape[1]
    held = 4
    mine = (owner_table == me).astype(jnp.int32)
    ids = jnp.arange(count, dtype=jnp.int32)
    before = jnp.sum(jnp.where(ids[None, :] < ids[:, None], mine[None, :], 0), axis=1)
    chosen = (mine[None, :] > 0) & (before[None, :] == jnp.arange(held, dtype=jnp.int32)[:, None])
    picked = jnp.sum(jnp.where(chosen, ids[None, :], 0), axis=1)
    lengths = jnp.sum(jnp.where(chosen, size_table[None, :], 0), axis=1)
    rows = index_table.at[picked].get(mode="promise_in_bounds")
    used = (jnp.arange(kmax, dtype=jnp.int32)[None, :] < lengths[:, None]).reshape(1, held * kmax)
    place = rows.reshape(held * kmax, 1) == jnp.arange(captions.shape[0], dtype=jnp.int32)[None, :]
    ordered = jnp.dot(place.astype(bf16), captions, preferred_element_type=f32).astype(bf16)
    return ordered, used


def by_rows(left, right):
    return lax.dot_general(left, right, (((0,), (0,)), ((), ())), preferred_element_type=f32)


vmem = pl.BlockSpec(memory_space=pltpu.VMEM)
smem = pl.BlockSpec(memory_space=pltpu.SMEM)
anywhere = pl.BlockSpec(memory_space=pl.ANY)


def call(kernel, out_shape, *operands, places=None, scratch=(), room=12):
    return pl.pallas_call(
        kernel,
        out_shape=out_shape,
        in_specs=places or [vmem] * len(operands),
        scratch_shapes=scratch,
        compiler_params=pltpu.CompilerParams(vmem_limit_bytes=room * 2**20),
    )(*operands)


def first_kernel(at_ref, weight_ref, out_ref):
    block = out_ref.shape[2]
    value = weight_ref[:, pl.ds(pl.multiple_of(at_ref[0] * block, block), block)]
    out_ref[...] = jnp.broadcast_to(value[None], out_ref.shape)


def partial_kernel(parts, at_ref, own_ref, sent_ref, *refs):
    blocks, (own_out, other_out, weight_out, here, sems) = refs[:parts], refs[parts:]
    copies = [pltpu.make_async_copy(blocks[i], here.at[i], sems.at[i]) for i in range(parts)]
    for copy in copies:
        copy.start()
    own, sent = own_ref[...], sent_ref[...]
    for i in range(parts):
        width = here.shape[2]
        columns = pl.ds(pl.multiple_of((at_ref[0] ^ i) * width, width), width)
        copies[i].wait()
        block = here[i]
        other_out[:, columns] = by_rows(sent, block)
        own_out[:, columns] = by_rows(own, block)
        weight_out[:, columns] = block


def payload_kernel(own_ref, sent_ref, slots_ref, labels_ref, unit_ref, norm_ref, out_ref):
    projected = own_ref[...] + sent_ref[...]
    norm_len = jnp.sqrt(jnp.sum(projected * projected, axis=1, keepdims=True) + 1e-06)
    unit = projected / norm_len
    unit_ref[...] = unit
    norm_ref[...] = norm_len
    rows, width = out_ref.shape[0], unit.shape[1]
    here = lax.broadcasted_iota(jnp.int32, (rows, unit.shape[0]), 0) == slots_ref[...]
    place = jnp.where(here, 1.0, 0.0).astype(bf16)
    out_ref[:, :width] = jnp.dot(place, unit.astype(bf16), preferred_element_type=f32).astype(bf16)
    out_ref[:, width:] = jnp.dot(place, labels_ref[...], preferred_element_type=f32).astype(bf16)


def sum_kernel(depth, pieces_ref, out_ref):
    size = out_ref.shape[1]
    total = pieces_ref[0].astype(f32)
    for i in range(1, pieces_ref.shape[0]):
        total += pieces_ref[i].astype(f32)
    tail = total[size - 2 * depth :]
    tail = tail + pltpu.roll(tail, depth, 0)
    for i in range(out_ref.shape[0]):
        out_ref[i, : size - 2 * depth, :] = total[: size - 2 * depth]
        out_ref[i, size - 2 * depth :, :] = tail


def last_kernel(depth, at_ref, last_ref, weight_ref, gain_ref, bias_ref):
    group, _, block = last_ref.shape
    shard, width = weight_ref.shape
    cores = group * block // width
    for i in range(width // block):
        weight_ref[:, i * block : (i + 1) * block] = last_ref[i * cores + at_ref[1], :shard, :]
    for i in range(group // 2):
        gain_ref[i * depth : (i + 1) * depth, :] = last_ref[i, shard : shard + depth, :]
        bias_ref[i * depth : (i + 1) * depth, :] = last_ref[i + group // 2, shard : shard + depth, :]


def owner_kernel(kmax, parts, rows_ref, ordered_ref, used_ref, out_ref):
    count, (held, width) = rows_ref.shape[0], ordered_ref.shape
    block = width // parts
    ordered = ordered_ref[...]
    labels = rows_ref[:, width:].astype(f32).astype(jnp.int32)
    local, target = labels[:, 0:1], labels[:, 1:2]
    columns = lax.broadcasted_iota(jnp.int32, (count, held), 1)
    first = local * kmax
    valid = (used_ref[...] > 0) & (columns >= first) & (columns < first + kmax)
    scores = logit_scale * lax.dot_general(
        rows_ref[:, :width], ordered, (((1,), (1,)), ((), ())), preferred_element_type=f32
    )
    highest = jnp.max(jnp.where(valid, scores, -jnp.inf), axis=1, keepdims=True)
    weights = jnp.where(valid, jnp.exp(scores - highest), 0.0)
    probs = weights / jnp.sum(weights, axis=1, keepdims=True)
    positive = jnp.where(columns == first + target, 1.0, 0.0)
    coefficients = (logit_scale * (probs - positive)).astype(bf16)
    gradient = jnp.dot(coefficients, ordered, preferred_element_type=f32).astype(bf16)
    size = 16 * parts
    row = lax.broadcasted_iota(jnp.int32, (size, size), 0)
    column = lax.broadcasted_iota(jnp.int32, (size, size), 1)
    order = jnp.where(column == lax.rem(row, parts) * 16 + lax.div(row, parts), 1.0, 0.0).astype(bf16)
    for at in range(0, count, 16):
        some = jnp.concatenate([gradient[at : at + 16, i * block : (i + 1) * block] for i in range(parts)], axis=0)
        out_ref[at * parts : (at + 16) * parts, :] = jnp.dot(order, some, preferred_element_type=f32).astype(bf16)


def gradient_kernel(
    parts,
    depth,
    back_ref,
    slots_ref,
    unit_ref,
    norm_ref,
    cot_ref,
    weight_ref,
    normed_ref,
    pieces_ref,
    grad_ref,
    weight_here,
    normed_here,
    sems,
):
    group, rows, block = pieces_ref.shape
    count = unit_ref.shape[0]
    steps = sems.shape[1]
    step = weight_ref.shape[0] // steps
    copies = []
    for j in range(steps):
        some = pl.ds(j * step, step)
        copies.append(pltpu.make_async_copy(weight_ref.at[some, :], weight_here.at[some, :], sems.at[0, j]))
        copies.append(pltpu.make_async_copy(normed_ref.at[:, some], normed_here.at[:, some], sems.at[1, j]))
    for copy in copies:
        copy.start()
    back, unit, slots = back_ref[...], unit_ref[...], slots_ref[...]
    columns = lax.broadcasted_iota(jnp.int32, (count, back.shape[0]), 1)
    blocks = []
    for i in range(parts):
        here = jnp.where(columns == slots * parts + i, 1.0, 0.0).astype(bf16)
        blocks.append(jnp.dot(here, back, preferred_element_type=f32))
    unit_grad = cot_ref[...] * jnp.concatenate(blocks, axis=1)
    along = jnp.sum(unit * unit_grad, axis=1, keepdims=True)
    proj = ((unit_grad - unit * along) / norm_ref[...]).astype(bf16)
    gain, bias = [], []
    for j in range(steps):
        some = slice(j * step, (j + 1) * step)
        copies[2 * j].wait()
        part = lax.dot_general(
            proj, weight_here[some, :], (((1,), (1,)), ((), ())), preferred_element_type=f32
        )
        grad_ref[:, some] = part
        copies[2 * j + 1].wait()
        gain.append(jnp.sum(part * normed_here[:, some], axis=0, keepdims=True))
        bias.append(jnp.sum(part, axis=0, keepdims=True))
    place = lax.broadcasted_iota(jnp.int32, (rows - count, block), 0)
    for g in range(group):
        tail = jnp.zeros((rows - count, block), f32)
        values, at = (gain, g) if g < group // 2 else (bias, g - group // 2)
        for r in range(depth):
            begin = (at * depth + r) * block
            line = values[begin // step][:, begin % step : begin % step + block]
            high = line.astype(bf16).astype(f32)
            tail = jnp.where(place == r, high, jnp.where(place == depth + r, line - high, tail))
        i = g * parts // group
        pieces_ref[g, :count, :] = proj[:, i * block : (i + 1) * block]
        pieces_ref[g, count:, :] = tail.astype(bf16)


def term_kernel(windows_ref, pieces_ref, out_ref, here, total, sems):
    groups, _, width = windows_ref.shape
    count = width // 2
    copies = [pltpu.make_async_copy(windows_ref.at[g], here.at[g], sems.at[g]) for g in range(groups)]
    for copy in copies:
        copy.start()
    for g in range(groups):
        proj = jnp.concatenate([pieces_ref[2 * g, :count, :], pieces_ref[2 * g + 1, :count, :]], axis=0)
        copies[g].wait()
        product = jnp.dot(here[g], proj, preferred_element_type=f32)
        if g == 0:
            total[...] = product
        elif g < groups - 1:
            total[...] += product
        else:
            out_ref[...] = (total[...] + product).astype(bf16)


def body(
    feats,
    ln_gain,
    ln_bias,
    head_weight,
    captions,
    image_cluster,
    image_target,
    cluster_owner,
    cluster_size,
    cap_index,
    cotangent,
):
    count, width = feats.shape
    window_width = ln_gain.shape[0]
    embed_width = head_weight.shape[1]
    shard = head_weight.shape[0]
    nz, ny, nc = lax.axis_size("z"), lax.axis_size("y"), lax.axis_size("core")
    dp_count = nz * ny * nc
    half = window_width // nc
    core = lax.axis_index("core")
    me = lax.axis_index(DP)
    capacity = 2
    kmax = cap_index.shape[2]
    owner_table = cluster_owner[0]

    outer = lax.axis_index("outer")
    n_outer = lax.axis_size("outer")
    block = embed_width // n_outer
    at = jnp.stack([outer, core])
    columns = call(
        first_kernel,
        jax.ShapeDtypeStruct((nz * ny, shard, block), bf16),
        at,
        head_weight,
        places=[smem, vmem],
    )
    columns = exchange(columns, ("z", "y")).reshape(half, block)

    widened = feats.astype(f32)
    means = jnp.mean(widened, axis=1, keepdims=True)
    centred = widened - means
    inv_std = lax.rsqrt(jnp.mean(centred * centred, axis=1, keepdims=True) + 1e-05)
    normed_head = centred[:, :window_width] * inv_std
    normed_tail = centred[:, window_width:] * inv_std
    window_bf = (normed_head * ln_gain + ln_bias).astype(bf16)
    by_feature = window_bf.T.reshape(nz * ny, nc, shard, count)
    window_own = lax.dynamic_index_in_dim(by_feature, core, 1, keepdims=False).reshape(half, count)
    window_other = lax.dynamic_index_in_dim(by_feature, 1 - core, 1, keepdims=False).reshape(half, count)
    columns, window_other = lax.optimization_barrier((columns, window_other))
    blocks = [columns] + [swap(columns, "outer", i) for i in range(1, n_outer)]
    window_sent = swap(window_other, "core", 1)
    window_pair = jnp.concatenate(
        [jnp.where(core == 0, window_own, window_sent), jnp.where(core == 0, window_sent, window_own)], axis=1
    )
    ids = jnp.arange(owner_table.shape[0], dtype=jnp.int32)[None, :]
    owners = jnp.sum(jnp.where(image_cluster[:, None] == ids, owner_table[None, :], 0), axis=1)
    local = jnp.sum(
        ((owner_table[None, :] == owners[:, None]) & (ids < image_cluster[:, None])).astype(jnp.int32), axis=1
    )
    images = jnp.arange(count, dtype=jnp.int32)
    ranks = jnp.sum(
        ((owners[:, None] == owners[None, :]) & (images[None, :] < images[:, None])).astype(jnp.int32), axis=1
    )
    slots = owners * capacity + ranks
    labels = jnp.stack([local, image_target], axis=1).astype(bf16)
    labels = jnp.concatenate([labels, jnp.zeros((count, 126), bf16)], axis=1)
    ordered, used = owner_tables(captions, owner_table, cluster_size[0], cap_index[0], me)

    partial_own, partial_other, weight_own = call(
        functools.partial(partial_kernel, n_outer),
        (
            jax.ShapeDtypeStruct((count, embed_width), f32),
            jax.ShapeDtypeStruct((count, embed_width), f32),
            jax.ShapeDtypeStruct((half, embed_width), bf16),
        ),
        at,
        window_own,
        window_sent,
        *blocks,
        places=[smem] + [vmem] * 2 + [anywhere] * n_outer,
        scratch=[pltpu.VMEM((n_outer, half, block), bf16), pltpu.SemaphoreType.DMA((n_outer,))],
    )
    partial_sent = swap(partial_other, "core", 1)
    unit, norm_len, send_rows = call(
        payload_kernel,
        (
            jax.ShapeDtypeStruct((count, embed_width), f32),
            jax.ShapeDtypeStruct((count, 1), f32),
            jax.ShapeDtypeStruct((dp_count * capacity, embed_width + 128), bf16),
        ),
        partial_own,
        partial_sent,
        slots[None, :],
        labels,
    )
    send_rows = send_rows.reshape(dp_count, capacity, -1)

    send_rows, window_pair = lax.optimization_barrier((send_rows, window_pair))
    window_all = lax.all_gather(window_pair, "outer", axis=0)
    received = exchange(send_rows, DP)
    gradient = call(
        functools.partial(owner_kernel, kmax, n_outer),
        jax.ShapeDtypeStruct((dp_count * capacity * n_outer, block), bf16),
        received.reshape(dp_count * capacity, -1),
        ordered,
        used.astype(f32),
    )
    gradient, weight_own = lax.optimization_barrier((gradient, weight_own))
    weight_other = swap(weight_own, "core", 1)
    first = jnp.where(core == 0, weight_own, weight_other).reshape(nz * ny, 1, shard, embed_width)
    second = jnp.where(core == 0, weight_other, weight_own).reshape(nz * ny, 1, shard, embed_width)
    full_weight = jnp.concatenate([first, second], axis=1).reshape(window_width, embed_width)
    returned = exchange(gradient.reshape(dp_count, capacity * n_outer, block), DP).reshape(-1, block)

    group = n_outer * nc
    depth = 2 * window_width // (group * block)
    pieces, window_grad = call(
        functools.partial(gradient_kernel, n_outer, depth),
        (
            jax.ShapeDtypeStruct((group, count + 16, block), bf16),
            jax.ShapeDtypeStruct((count, window_width), f32),
        ),
        returned,
        slots[:, None],
        unit,
        norm_len,
        cotangent[:, None],
        full_weight,
        normed_head,
        places=[vmem] * 5 + [anywhere] * 2,
        scratch=[
            pltpu.VMEM((window_width, embed_width), bf16),
            pltpu.VMEM((count, window_width), f32),
            pltpu.SemaphoreType.DMA((2, 4)),
        ],
        room=50,
    )
    pieces = exchange(pieces, ("outer", "core"))
    sums = jnp.sum(pieces[:, count : count + 2 * depth].astype(f32), axis=0)
    sums = sums[:depth] + sums[depth:]

    term = call(
        term_kernel,
        jax.ShapeDtypeStruct((half, block), bf16),
        window_all,
        pieces,
        places=[anywhere, vmem],
        scratch=[
            pltpu.VMEM((n_outer, half, nc * count), bf16),
            pltpu.VMEM((half, block), f32),
            pltpu.SemaphoreType.DMA((n_outer,)),
        ],
        room=57,
    )
    sums = split_sum(sums, 0)
    sums = jnp.broadcast_to(sums[None], (nz * ny,) + sums.shape)
    pieces = exchange(jnp.concatenate([term.reshape(nz * ny, shard, block), sums], axis=1), ("z", "y"))

    pieces = call(
        functools.partial(sum_kernel, depth),
        jax.ShapeDtypeStruct((group, shard + 2 * depth, block), f32),
        pieces,
    )
    weight_grad, gain_grad, bias_grad = call(
        functools.partial(last_kernel, depth),
        (
            jax.ShapeDtypeStruct((shard, embed_width), f32),
            jax.ShapeDtypeStruct((window_width // block, block), f32),
            jax.ShapeDtypeStruct((window_width // block, block), f32),
        ),
        at,
        exchange(pieces, ("outer", "core")),
        places=[smem, vmem],
    )
    gain_grad, bias_grad = gain_grad.reshape(window_width), bias_grad.reshape(window_width)

    scaled_grad = window_grad * ln_gain
    first_mean = jnp.sum(scaled_grad, axis=1, keepdims=True) / width
    second_mean = jnp.sum(scaled_grad * normed_head, axis=1, keepdims=True) / width
    grad_head = inv_std * (scaled_grad - first_mean - normed_head * second_mean)
    grad_tail = inv_std * (0.0 - first_mean - normed_tail * second_mean)
    feat_grad = jnp.concatenate([grad_head.astype(bf16), grad_tail.astype(bf16)], axis=1)
    return (feat_grad, weight_grad, gain_grad, bias_grad)


def solution(mesh):
    outer, dp = mesh.devices.shape
    fine = Mesh(mesh.devices.reshape(outer, 8, dp // 16, 2), ALL)
    in_specs = (
        P(ALL, None),
        P(),
        P(),
        P(DP, None),
        P(ALL, None),
        P(ALL),
        P(ALL),
        P("outer", None),
        P("outer", None),
        P("outer", None, None),
        P(ALL),
    )
    out_specs = (P(ALL, None), P(DP, None), P(), P())
    return jax.shard_map(body, mesh=fine, in_specs=in_specs, out_specs=out_specs, check_vma=False)
```

```python
import functools

import jax
import jax.numpy as jnp
from jax import lax
from jax.experimental import pallas as pl
from jax.experimental.pallas import tpu as pltpu
from jax.sharding import Mesh, PartitionSpec as P

logit_scale = 100.0
bf16 = jnp.bfloat16
f32 = jnp.float32
DP = ("z", "y", "core")
ALL = ("outer", "z", "y", "core")


def swap(value, axis, flip):
    size = lax.axis_size(axis)
    return lax.ppermute(value, axis, [(i, i ^ flip) for i in range(size)])


def split_sum(value, axis):
    high = lax.reduce_precision(value, 8, 7)
    return jnp.concatenate([high.astype(bf16), (value - high).astype(bf16)], axis=axis)


def exchange(pieces, axis):
    return lax.all_to_all(pieces, axis, split_axis=0, concat_axis=0, tiled=True)


def gather(value, axis):
    size = lax.axis_size(axis)
    return exchange(jnp.broadcast_to(value[None], (size,) + value.shape), axis)


def side_by_side(blocks):
    return jnp.concatenate([blocks[i] for i in range(blocks.shape[0])], axis=1)


def owner_tables(captions, owner_table, size_table, index_table, me):
    count = owner_table.shape[0]
    kmax = index_table.shape[1]
    held = 4
    mine = (owner_table == me).astype(jnp.int32)
    ids = jnp.arange(count, dtype=jnp.int32)
    before = jnp.sum(jnp.where(ids[None, :] < ids[:, None], mine[None, :], 0), axis=1)
    chosen = (mine[None, :] > 0) & (before[None, :] == jnp.arange(held, dtype=jnp.int32)[:, None])
    picked = jnp.sum(jnp.where(chosen, ids[None, :], 0), axis=1)
    lengths = jnp.sum(jnp.where(chosen, size_table[None, :], 0), axis=1)
    rows = index_table.at[picked].get(mode="promise_in_bounds")
    used = (jnp.arange(kmax, dtype=jnp.int32)[None, :] < lengths[:, None]).reshape(1, held * kmax)
    place = rows.reshape(held * kmax, 1) == jnp.arange(captions.shape[0], dtype=jnp.int32)[None, :]
    ordered = jnp.dot(place.astype(bf16), captions, preferred_element_type=f32).astype(bf16)
    return ordered, used


vmem = pl.BlockSpec(memory_space=pltpu.VMEM)
smem = pl.BlockSpec(memory_space=pltpu.SMEM)


def call(kernel, out_shape, *operands, places=None):
    return pl.pallas_call(
        kernel,
        out_shape=out_shape,
        in_specs=places or [vmem] * len(operands),
        compiler_params=pltpu.CompilerParams(vmem_limit_bytes=12 * 2**20),
    )(*operands)


def owner_kernel(kmax, parts, rows_ref, ordered_ref, used_ref, out_ref):
    count, (held, width) = rows_ref.shape[0], ordered_ref.shape
    block = width // parts
    ordered = ordered_ref[...]
    labels = rows_ref[:, width:].astype(f32).astype(jnp.int32)
    local, target = labels[:, 0:1], labels[:, 1:2]
    columns = lax.broadcasted_iota(jnp.int32, (count, held), 1)
    first = local * kmax
    valid = (used_ref[...] > 0) & (columns >= first) & (columns < first + kmax)
    scores = logit_scale * lax.dot_general(
        rows_ref[:, :width], ordered, (((1,), (1,)), ((), ())), preferred_element_type=f32
    )
    highest = jnp.max(jnp.where(valid, scores, -jnp.inf), axis=1, keepdims=True)
    weights = jnp.where(valid, jnp.exp(scores - highest), 0.0)
    probs = weights / jnp.sum(weights, axis=1, keepdims=True)
    positive = jnp.where(columns == first + target, 1.0, 0.0)
    coefficients = (logit_scale * (probs - positive)).astype(bf16)
    gradient = jnp.dot(coefficients, ordered, preferred_element_type=f32).astype(bf16)
    size = 16 * parts
    row = lax.broadcasted_iota(jnp.int32, (size, size), 0)
    column = lax.broadcasted_iota(jnp.int32, (size, size), 1)
    order = jnp.where(column == lax.rem(row, parts) * 16 + lax.div(row, parts), 1.0, 0.0).astype(bf16)
    for at in range(0, count, 16):
        some = jnp.concatenate([gradient[at : at + 16, i * block : (i + 1) * block] for i in range(parts)], axis=0)
        out_ref[at * parts : (at + 16) * parts, :] = jnp.dot(order, some, preferred_element_type=f32).astype(bf16)


def sum_kernel(depth, pieces_ref, out_ref):
    size = out_ref.shape[1]
    total = pieces_ref[0].astype(f32)
    for i in range(1, pieces_ref.shape[0]):
        total += pieces_ref[i].astype(f32)
    tail = total[size - 2 * depth :]
    tail = tail + pltpu.roll(tail, depth, 0)
    for i in range(out_ref.shape[0]):
        out_ref[i, : size - 2 * depth, :] = total[: size - 2 * depth]
        out_ref[i, size - 2 * depth :, :] = tail


def last_kernel(depth, at_ref, last_ref, weight_ref, gain_ref, bias_ref):
    group, _, block = last_ref.shape
    shard, width = weight_ref.shape
    cores = group * block // width
    for i in range(width // block):
        weight_ref[:, i * block : (i + 1) * block] = last_ref[i * cores + at_ref[1], :shard, :]
    for i in range(group // 2):
        gain_ref[i * depth : (i + 1) * depth, :] = last_ref[i, shard : shard + depth, :]
        bias_ref[i * depth : (i + 1) * depth, :] = last_ref[i + group // 2, shard : shard + depth, :]


def owner_kernel(kmax, parts, rows_ref, ordered_ref, used_ref, out_ref):
    count, (held, width) = rows_ref.shape[0], ordered_ref.shape
    block = width // parts
    ordered = ordered_ref[...]
    labels = rows_ref[:, width:].astype(f32).astype(jnp.int32)
    local, target = labels[:, 0:1], labels[:, 1:2]
    columns = lax.broadcasted_iota(jnp.int32, (count, held), 1)
    first = local * kmax
    valid = (used_ref[...] > 0) & (columns >= first) & (columns < first + kmax)
    scores = logit_scale * lax.dot_general(
        rows_ref[:, :width], ordered, (((1,), (1,)), ((), ())), preferred_element_type=f32
    )
    highest = jnp.max(jnp.where(valid, scores, -jnp.inf), axis=1, keepdims=True)
    weights = jnp.where(valid, jnp.exp(scores - highest), 0.0)
    probs = weights / jnp.sum(weights, axis=1, keepdims=True)
    positive = jnp.where(columns == first + target, 1.0, 0.0)
    coefficients = (logit_scale * (probs - positive)).astype(bf16)
    gradient = jnp.dot(coefficients, ordered, preferred_element_type=f32).astype(bf16)
    size = 16 * parts
    row = lax.broadcasted_iota(jnp.int32, (size, size), 0)
    column = lax.broadcasted_iota(jnp.int32, (size, size), 1)
    order = jnp.where(column == lax.rem(row, parts) * 16 + lax.div(row, parts), 1.0, 0.0).astype(bf16)
    for at in range(0, count, 16):
        some = jnp.concatenate([gradient[at : at + 16, i * block : (i + 1) * block] for i in range(parts)], axis=0)
        out_ref[at * parts : (at + 16) * parts, :] = jnp.dot(order, some, preferred_element_type=f32).astype(bf16)


def gradient_kernel(
    parts, depth, back_ref, slots_ref, unit_ref, norm_ref, cot_ref, weight_ref, normed_ref, pieces_ref, grad_ref
):
    group, rows, block = pieces_ref.shape
    count = unit_ref.shape[0]
    back, unit, slots = back_ref[...], unit_ref[...], slots_ref[...]
    columns = lax.broadcasted_iota(jnp.int32, (count, back.shape[0]), 1)
    blocks = []
    for i in range(parts):
        here = jnp.where(columns == slots * parts + i, 1.0, 0.0).astype(bf16)
        blocks.append(jnp.dot(here, back, preferred_element_type=f32))
    unit_grad = cot_ref[...] * jnp.concatenate(blocks, axis=1)
    along = jnp.sum(unit * unit_grad, axis=1, keepdims=True)
    proj = ((unit_grad - unit * along) / norm_ref[...]).astype(bf16)
    window_grad = lax.dot_general(
        proj, weight_ref[...], (((1,), (1,)), ((), ())), preferred_element_type=f32
    )
    grad_ref[...] = window_grad
    gain = jnp.sum(window_grad * normed_ref[...], axis=0, keepdims=True)
    bias = jnp.sum(window_grad, axis=0, keepdims=True)
    place = lax.broadcasted_iota(jnp.int32, (rows - count, block), 0)
    for g in range(group):
        tail = jnp.zeros((rows - count, block), f32)
        values, at = (gain, g) if g < group // 2 else (bias, g - group // 2)
        for r in range(depth):
            line = values[:, (at * depth + r) * block : (at * depth + r + 1) * block]
            high = line.astype(bf16).astype(f32)
            tail = jnp.where(place == r, high, jnp.where(place == depth + r, line - high, tail))
        i = g * parts // group
        pieces_ref[g, :count, :] = proj[:, i * block : (i + 1) * block]
        pieces_ref[g, count:, :] = tail.astype(bf16)


def term_kernel(windows_ref, pieces_ref, out_ref):
    groups, height, width = windows_ref.shape
    count = width // 2
    step = height // 4
    proj = [
        jnp.concatenate([pieces_ref[2 * g, :count, :], pieces_ref[2 * g + 1, :count, :]], axis=0)
        for g in range(groups)
    ]
    for at in range(0, height, step):
        total = jnp.dot(windows_ref[0, at : at + step, :], proj[0], preferred_element_type=f32)
        for g in range(1, groups):
            total += jnp.dot(windows_ref[g, at : at + step, :], proj[g], preferred_element_type=f32)
        out_ref[at : at + step, :] = total.astype(bf16)


def body(
    feats,
    ln_gain,
    ln_bias,
    head_weight,
    captions,
    image_cluster,
    image_target,
    cluster_owner,
    cluster_size,
    cap_index,
    cotangent,
):
    count, width = feats.shape
    window_width = ln_gain.shape[0]
    embed_width = head_weight.shape[1]
    shard = head_weight.shape[0]
    nz, ny, nc = lax.axis_size("z"), lax.axis_size("y"), lax.axis_size("core")
    dp_count = nz * ny * nc
    half = window_width // nc
    core = lax.axis_index("core")
    me = lax.axis_index(DP)
    capacity = 2
    kmax = cap_index.shape[2]
    owner_table = cluster_owner[0]

    outer = lax.axis_index("outer")
    n_outer = lax.axis_size("outer")
    block = embed_width // n_outer
    columns = lax.dynamic_slice_in_dim(head_weight, outer * block, block, 1)
    columns = gather(columns, ("z", "y")).reshape(half, block)
    weight_own = side_by_side(gather(columns, "outer"))

    widened = feats.astype(f32)
    means = jnp.mean(widened, axis=1, keepdims=True)
    centred = widened - means
    inv_std = lax.rsqrt(jnp.mean(centred * centred, axis=1, keepdims=True) + 1e-05)
    normed_head = centred[:, :window_width] * inv_std
    normed_tail = centred[:, window_width:] * inv_std
    window_bf = (normed_head * ln_gain + ln_bias).astype(bf16)
    by_feature = window_bf.T.reshape(nz * ny, nc, shard, count)
    window_own = lax.dynamic_index_in_dim(by_feature, core, 1, keepdims=False).reshape(half, count)
    window_other = lax.dynamic_index_in_dim(by_feature, 1 - core, 1, keepdims=False).reshape(half, count)
    window_sent = swap(window_other, "core", 1)
    window_pair = jnp.concatenate(
        [jnp.where(core == 0, window_own, window_sent), jnp.where(core == 0, window_sent, window_own)], axis=1
    )

    ids = jnp.arange(owner_table.shape[0], dtype=jnp.int32)[None, :]
    owners = jnp.sum(jnp.where(image_cluster[:, None] == ids, owner_table[None, :], 0), axis=1)
    local = jnp.sum(
        ((owner_table[None, :] == owners[:, None]) & (ids < image_cluster[:, None])).astype(jnp.int32), axis=1
    )
    images = jnp.arange(count, dtype=jnp.int32)
    ranks = jnp.sum(
        ((owners[:, None] == owners[None, :]) & (images[None, :] < images[:, None])).astype(jnp.int32), axis=1
    )
    slots = owners * capacity + ranks
    place = (jnp.arange(dp_count * capacity, dtype=jnp.int32)[:, None] == slots[None, :]).astype(bf16)
    labels = jnp.stack([local, image_target], axis=1).astype(bf16)
    labels = jnp.concatenate([labels, jnp.zeros((count, 126), bf16)], axis=1)
    ordered, used = owner_tables(captions, owner_table, cluster_size[0], cap_index[0], me)

    def by_rows(left, right):
        return lax.dot_general(left, right, (((0,), (0,)), ((), ())), preferred_element_type=f32)

    weight_own, window_pair = lax.optimization_barrier((weight_own, window_pair))
    window_all = lax.all_gather(window_pair, "outer", axis=0)

    partial = by_rows(window_pair, weight_own).reshape(nc, count, embed_width)
    partial_own = lax.dynamic_index_in_dim(partial, core, 0, keepdims=False)
    partial_other = lax.dynamic_index_in_dim(partial, 1 - core, 0, keepdims=False)
    partial_sent = swap(partial_other, "core", 1)
    projected = partial_own + partial_sent
    weight_other = swap(weight_own, "core", 1)
    first = jnp.where(core == 0, weight_own, weight_other).reshape(nz * ny, 1, shard, embed_width)
    second = jnp.where(core == 0, weight_other, weight_own).reshape(nz * ny, 1, shard, embed_width)
    full_weight = jnp.concatenate([first, second], axis=1).reshape(window_width, embed_width)
    norm_len = jnp.sqrt(jnp.sum(projected * projected, axis=1, keepdims=True) + 1e-06)
    unit = projected / norm_len
    payload = jnp.concatenate([unit.astype(bf16), labels], axis=1)
    send_rows = jnp.dot(place, payload, preferred_element_type=f32).astype(bf16)
    received = lax.all_to_all(
        send_rows.reshape(dp_count, capacity, -1), DP, split_axis=0, concat_axis=0, tiled=True
    )
    gradient = call(
        functools.partial(owner_kernel, kmax, n_outer),
        jax.ShapeDtypeStruct((dp_count * capacity * n_outer, block), bf16),
        received.reshape(dp_count * capacity, -1),
        ordered,
        used.astype(f32),
    )
    returned = exchange(gradient.reshape(dp_count, capacity * n_outer, block), DP).reshape(-1, block)

    group = n_outer * nc
    depth = 2 * window_width // (group * block)
    pieces, window_grad = call(
        functools.partial(gradient_kernel, n_outer, depth),
        (
            jax.ShapeDtypeStruct((group, count + 16, block), bf16),
            jax.ShapeDtypeStruct((count, window_width), f32),
        ),
        returned,
        slots[:, None],
        unit,
        norm_len,
        cotangent[:, None],
        full_weight,
        normed_head,
    )
    pieces = exchange(pieces, ("outer", "core"))
    sums = jnp.sum(pieces[:, count : count + 2 * depth].astype(f32), axis=0)
    sums = sums[:depth] + sums[depth:]

    term = call(term_kernel, jax.ShapeDtypeStruct((half, block), bf16), window_all, pieces)
    sums = split_sum(sums, 0)
    sums = jnp.broadcast_to(sums[None], (nz * ny,) + sums.shape)
    pieces = exchange(jnp.concatenate([term.reshape(nz * ny, shard, block), sums], axis=1), ("z", "y"))

    pieces = call(
        functools.partial(sum_kernel, depth),
        jax.ShapeDtypeStruct((group, shard + 2 * depth, block), f32),
        pieces,
    )
    weight_grad, gain_grad, bias_grad = call(
        functools.partial(last_kernel, depth),
        (
            jax.ShapeDtypeStruct((shard, embed_width), f32),
            jax.ShapeDtypeStruct((window_width // block, block), f32),
            jax.ShapeDtypeStruct((window_width // block, block), f32),
        ),
        jnp.stack([outer, core]),
        exchange(pieces, ("outer", "core")),
        places=[smem, vmem],
    )
    gain_grad, bias_grad = gain_grad.reshape(window_width), bias_grad.reshape(window_width)

    scaled_grad = window_grad * ln_gain
    first_mean = jnp.sum(scaled_grad, axis=1, keepdims=True) / width
    second_mean = jnp.sum(scaled_grad * normed_head, axis=1, keepdims=True) / width
    grad_head = inv_std * (scaled_grad - first_mean - normed_head * second_mean)
    grad_tail = inv_std * (0.0 - first_mean - normed_tail * second_mean)
    feat_grad = jnp.concatenate([grad_head.astype(bf16), grad_tail.astype(bf16)], axis=1)
    return (feat_grad, weight_grad, gain_grad, bias_grad)


def solution(mesh):
    outer, dp = mesh.devices.shape
    fine = Mesh(mesh.devices.reshape(outer, 8, dp // 16, 2), ALL)
    in_specs = (
        P(ALL, None),
        P(),
        P(),
        P(DP, None),
        P(ALL, None),
        P(ALL),
        P(ALL),
        P("outer", None),
        P("outer", None),
        P("outer", None, None),
        P(ALL),
    )
    out_specs = (P(ALL, None), P(DP, None), P(), P())
    return jax.shard_map(body, mesh=fine, in_specs=in_specs, out_specs=out_specs, check_vma=False)
```

```python
import functools

import jax
import jax.numpy as jnp
from jax import lax
from jax.experimental import pallas as pl
from jax.experimental.pallas import tpu as pltpu
from jax.sharding import Mesh, PartitionSpec as P

logit_scale = 100.0
bf16 = jnp.bfloat16
f32 = jnp.float32
DP = ("z", "y", "core")
ALL = ("outer", "z", "y", "core")


def swap(value, axis, flip):
    size = lax.axis_size(axis)
    return lax.ppermute(value, axis, [(i, i ^ flip) for i in range(size)])


def split_sum(value, axis):
    high = lax.reduce_precision(value, 8, 7)
    return jnp.concatenate([high.astype(bf16), (value - high).astype(bf16)], axis=axis)


def exchange(pieces, axis):
    return lax.all_to_all(pieces, axis, split_axis=0, concat_axis=0, tiled=True)


def gather(value, axis):
    size = lax.axis_size(axis)
    return exchange(jnp.broadcast_to(value[None], (size,) + value.shape), axis)


def side_by_side(blocks):
    return jnp.concatenate([blocks[i] for i in range(blocks.shape[0])], axis=1)


def owner_tables(captions, owner_table, size_table, index_table, me):
    count = owner_table.shape[0]
    kmax = index_table.shape[1]
    held = 4
    mine = (owner_table == me).astype(jnp.int32)
    ids = jnp.arange(count, dtype=jnp.int32)
    before = jnp.sum(jnp.where(ids[None, :] < ids[:, None], mine[None, :], 0), axis=1)
    chosen = (mine[None, :] > 0) & (before[None, :] == jnp.arange(held, dtype=jnp.int32)[:, None])
    picked = jnp.sum(jnp.where(chosen, ids[None, :], 0), axis=1)
    lengths = jnp.sum(jnp.where(chosen, size_table[None, :], 0), axis=1)
    rows = index_table.at[picked].get(mode="promise_in_bounds")
    used = (jnp.arange(kmax, dtype=jnp.int32)[None, :] < lengths[:, None]).reshape(1, held * kmax)
    place = rows.reshape(held * kmax, 1) == jnp.arange(captions.shape[0], dtype=jnp.int32)[None, :]
    ordered = jnp.dot(place.astype(bf16), captions, preferred_element_type=f32).astype(bf16)
    return ordered, used


vmem = pl.BlockSpec(memory_space=pltpu.VMEM)
smem = pl.BlockSpec(memory_space=pltpu.SMEM)


def call(kernel, out_shape, *operands, places=None):
    return pl.pallas_call(
        kernel,
        out_shape=out_shape,
        in_specs=places or [vmem] * len(operands),
        compiler_params=pltpu.CompilerParams(vmem_limit_bytes=12 * 2**20),
    )(*operands)


def owner_kernel(kmax, parts, rows_ref, ordered_ref, used_ref, out_ref):
    count, (held, width) = rows_ref.shape[0], ordered_ref.shape
    block = width // parts
    ordered = ordered_ref[...]
    labels = rows_ref[:, width:].astype(f32).astype(jnp.int32)
    local, target = labels[:, 0:1], labels[:, 1:2]
    columns = lax.broadcasted_iota(jnp.int32, (count, held), 1)
    first = local * kmax
    valid = (used_ref[...] > 0) & (columns >= first) & (columns < first + kmax)
    scores = logit_scale * lax.dot_general(
        rows_ref[:, :width], ordered, (((1,), (1,)), ((), ())), preferred_element_type=f32
    )
    highest = jnp.max(jnp.where(valid, scores, -jnp.inf), axis=1, keepdims=True)
    weights = jnp.where(valid, jnp.exp(scores - highest), 0.0)
    probs = weights / jnp.sum(weights, axis=1, keepdims=True)
    positive = jnp.where(columns == first + target, 1.0, 0.0)
    coefficients = (logit_scale * (probs - positive)).astype(bf16)
    gradient = jnp.dot(coefficients, ordered, preferred_element_type=f32).astype(bf16)
    size = 16 * parts
    row = lax.broadcasted_iota(jnp.int32, (size, size), 0)
    column = lax.broadcasted_iota(jnp.int32, (size, size), 1)
    order = jnp.where(column == lax.rem(row, parts) * 16 + lax.div(row, parts), 1.0, 0.0).astype(bf16)
    for at in range(0, count, 16):
        some = jnp.concatenate([gradient[at : at + 16, i * block : (i + 1) * block] for i in range(parts)], axis=0)
        out_ref[at * parts : (at + 16) * parts, :] = jnp.dot(order, some, preferred_element_type=f32).astype(bf16)


def sum_kernel(depth, pieces_ref, out_ref):
    size = out_ref.shape[1]
    total = pieces_ref[0].astype(f32)
    for i in range(1, pieces_ref.shape[0]):
        total += pieces_ref[i].astype(f32)
    tail = total[size - 2 * depth :]
    tail = tail + pltpu.roll(tail, depth, 0)
    for i in range(out_ref.shape[0]):
        out_ref[i, : size - 2 * depth, :] = total[: size - 2 * depth]
        out_ref[i, size - 2 * depth :, :] = tail


def last_kernel(depth, at_ref, last_ref, weight_ref, gain_ref, bias_ref):
    group, _, block = last_ref.shape
    shard, width = weight_ref.shape
    cores = group * block // width
    for i in range(width // block):
        weight_ref[:, i * block : (i + 1) * block] = last_ref[i * cores + at_ref[1], :shard, :]
    for i in range(group // 2):
        gain_ref[i * depth : (i + 1) * depth, :] = last_ref[i, shard : shard + depth, :]
        bias_ref[i * depth : (i + 1) * depth, :] = last_ref[i + group // 2, shard : shard + depth, :]


def owner_kernel(kmax, parts, rows_ref, ordered_ref, used_ref, out_ref):
    count, (held, width) = rows_ref.shape[0], ordered_ref.shape
    block = width // parts
    ordered = ordered_ref[...]
    labels = rows_ref[:, width:].astype(f32).astype(jnp.int32)
    local, target = labels[:, 0:1], labels[:, 1:2]
    columns = lax.broadcasted_iota(jnp.int32, (count, held), 1)
    first = local * kmax
    valid = (used_ref[...] > 0) & (columns >= first) & (columns < first + kmax)
    scores = logit_scale * lax.dot_general(
        rows_ref[:, :width], ordered, (((1,), (1,)), ((), ())), preferred_element_type=f32
    )
    highest = jnp.max(jnp.where(valid, scores, -jnp.inf), axis=1, keepdims=True)
    weights = jnp.where(valid, jnp.exp(scores - highest), 0.0)
    probs = weights / jnp.sum(weights, axis=1, keepdims=True)
    positive = jnp.where(columns == first + target, 1.0, 0.0)
    coefficients = (logit_scale * (probs - positive)).astype(bf16)
    gradient = jnp.dot(coefficients, ordered, preferred_element_type=f32).astype(bf16)
    size = 16 * parts
    row = lax.broadcasted_iota(jnp.int32, (size, size), 0)
    column = lax.broadcasted_iota(jnp.int32, (size, size), 1)
    order = jnp.where(column == lax.rem(row, parts) * 16 + lax.div(row, parts), 1.0, 0.0).astype(bf16)
    for at in range(0, count, 16):
        some = jnp.concatenate([gradient[at : at + 16, i * block : (i + 1) * block] for i in range(parts)], axis=0)
        out_ref[at * parts : (at + 16) * parts, :] = jnp.dot(order, some, preferred_element_type=f32).astype(bf16)


def gradient_kernel(
    parts, depth, back_ref, slots_ref, unit_ref, norm_ref, cot_ref, weight_ref, normed_ref, pieces_ref, grad_ref
):
    group, rows, block = pieces_ref.shape
    count = unit_ref.shape[0]
    back, unit, slots = back_ref[...], unit_ref[...], slots_ref[...]
    columns = lax.broadcasted_iota(jnp.int32, (count, back.shape[0]), 1)
    blocks = []
    for i in range(parts):
        here = jnp.where(columns == slots * parts + i, 1.0, 0.0).astype(bf16)
        blocks.append(jnp.dot(here, back, preferred_element_type=f32))
    unit_grad = cot_ref[...] * jnp.concatenate(blocks, axis=1)
    along = jnp.sum(unit * unit_grad, axis=1, keepdims=True)
    proj = ((unit_grad - unit * along) / norm_ref[...]).astype(bf16)
    window_grad = lax.dot_general(
        proj, weight_ref[...], (((1,), (1,)), ((), ())), preferred_element_type=f32
    )
    grad_ref[...] = window_grad
    gain = jnp.sum(window_grad * normed_ref[...], axis=0, keepdims=True)
    bias = jnp.sum(window_grad, axis=0, keepdims=True)
    place = lax.broadcasted_iota(jnp.int32, (rows - count, block), 0)
    for g in range(group):
        tail = jnp.zeros((rows - count, block), f32)
        values, at = (gain, g) if g < group // 2 else (bias, g - group // 2)
        for r in range(depth):
            line = values[:, (at * depth + r) * block : (at * depth + r + 1) * block]
            high = line.astype(bf16).astype(f32)
            tail = jnp.where(place == r, high, jnp.where(place == depth + r, line - high, tail))
        i = g * parts // group
        pieces_ref[g, :count, :] = proj[:, i * block : (i + 1) * block]
        pieces_ref[g, count:, :] = tail.astype(bf16)


def term_kernel(windows_ref, pieces_ref, out_ref):
    groups, height, width = windows_ref.shape
    count = width // 2
    step = height // 4
    proj = [
        jnp.concatenate([pieces_ref[2 * g, :count, :], pieces_ref[2 * g + 1, :count, :]], axis=0)
        for g in range(groups)
    ]
    for at in range(0, height, step):
        total = jnp.dot(windows_ref[0, at : at + step, :], proj[0], preferred_element_type=f32)
        for g in range(1, groups):
            total += jnp.dot(windows_ref[g, at : at + step, :], proj[g], preferred_element_type=f32)
        out_ref[at : at + step, :] = total.astype(bf16)


def body(
    feats,
    ln_gain,
    ln_bias,
    head_weight,
    captions,
    image_cluster,
    image_target,
    cluster_owner,
    cluster_size,
    cap_index,
    cotangent,
):
    count, width = feats.shape
    window_width = ln_gain.shape[0]
    embed_width = head_weight.shape[1]
    shard = head_weight.shape[0]
    nz, ny, nc = lax.axis_size("z"), lax.axis_size("y"), lax.axis_size("core")
    dp_count = nz * ny * nc
    half = window_width // nc
    core = lax.axis_index("core")
    me = lax.axis_index(DP)
    capacity = 2
    kmax = cap_index.shape[2]
    owner_table = cluster_owner[0]

    outer = lax.axis_index("outer")
    n_outer = lax.axis_size("outer")
    block = embed_width // n_outer
    columns = lax.dynamic_slice_in_dim(head_weight, outer * block, block, 1)
    columns = gather(columns, ("z", "y")).reshape(half, block)
    blocks = gather(columns, "outer")

    widened = feats.astype(f32)
    means = jnp.mean(widened, axis=1, keepdims=True)
    centred = widened - means
    inv_std = lax.rsqrt(jnp.mean(centred * centred, axis=1, keepdims=True) + 1e-05)
    normed_head = centred[:, :window_width] * inv_std
    normed_tail = centred[:, window_width:] * inv_std
    window_bf = (normed_head * ln_gain + ln_bias).astype(bf16)
    by_feature = window_bf.T.reshape(nz * ny, nc, shard, count)
    window_own = lax.dynamic_index_in_dim(by_feature, core, 1, keepdims=False).reshape(half, count)
    window_other = lax.dynamic_index_in_dim(by_feature, 1 - core, 1, keepdims=False).reshape(half, count)
    window_sent = swap(window_other, "core", 1)
    window_pair = jnp.concatenate(
        [jnp.where(core == 0, window_own, window_sent), jnp.where(core == 0, window_sent, window_own)], axis=1
    )

    ids = jnp.arange(owner_table.shape[0], dtype=jnp.int32)[None, :]
    owners = jnp.sum(jnp.where(image_cluster[:, None] == ids, owner_table[None, :], 0), axis=1)
    local = jnp.sum(
        ((owner_table[None, :] == owners[:, None]) & (ids < image_cluster[:, None])).astype(jnp.int32), axis=1
    )
    images = jnp.arange(count, dtype=jnp.int32)
    ranks = jnp.sum(
        ((owners[:, None] == owners[None, :]) & (images[None, :] < images[:, None])).astype(jnp.int32), axis=1
    )
    slots = owners * capacity + ranks
    labels = jnp.stack([local, image_target], axis=1).astype(bf16)
    labels = jnp.concatenate([labels, jnp.zeros((count, 126), bf16)], axis=1)
    ordered, used = owner_tables(captions, owner_table, cluster_size[0], cap_index[0], me)

    def by_rows(left, right):
        return lax.dot_general(left, right, (((0,), (0,)), ((), ())), preferred_element_type=f32)

    blocks, window_pair, slots, labels = lax.optimization_barrier((blocks, window_pair, slots, labels))
    place = (jnp.arange(dp_count * capacity, dtype=jnp.int32)[:, None] == slots[None, :]).astype(bf16)

    partial = by_rows(window_pair, side_by_side(blocks)).reshape(nc, count, embed_width)
    partial_own = lax.dynamic_index_in_dim(partial, core, 0, keepdims=False)
    partial_other = lax.dynamic_index_in_dim(partial, 1 - core, 0, keepdims=False)
    partial_sent = swap(partial_other, "core", 1)
    projected = partial_own + partial_sent
    blocks, window_pair, projected = lax.optimization_barrier((blocks, window_pair, projected))
    weight_all = lax.all_gather(blocks, "core", axis=0)
    window_all = lax.all_gather(window_pair, "outer", axis=0)
    norm_len = jnp.sqrt(jnp.sum(projected * projected, axis=1, keepdims=True) + 1e-06)
    unit = projected / norm_len
    payload = jnp.concatenate([unit.astype(bf16), labels], axis=1)
    send_rows = jnp.dot(place, payload, preferred_element_type=f32).astype(bf16)
    received = lax.all_to_all(
        send_rows.reshape(dp_count, capacity, -1), DP, split_axis=0, concat_axis=0, tiled=True
    )
    gradient = call(
        functools.partial(owner_kernel, kmax, n_outer),
        jax.ShapeDtypeStruct((dp_count * capacity * n_outer, block), bf16),
        received.reshape(dp_count * capacity, -1),
        ordered,
        used.astype(f32),
    )
    weight_all = [side_by_side(weight_all[i]).reshape(nz * ny, 1, shard, embed_width) for i in range(nc)]
    full_weight = jnp.concatenate(weight_all, axis=1).reshape(window_width, embed_width)
    returned = exchange(gradient.reshape(dp_count, capacity * n_outer, block), DP).reshape(-1, block)

    group = n_outer * nc
    depth = 2 * window_width // (group * block)
    pieces, window_grad = call(
        functools.partial(gradient_kernel, n_outer, depth),
        (
            jax.ShapeDtypeStruct((group, count + 16, block), bf16),
            jax.ShapeDtypeStruct((count, window_width), f32),
        ),
        returned,
        slots[:, None],
        unit,
        norm_len,
        cotangent[:, None],
        full_weight,
        normed_head,
    )
    pieces = exchange(pieces, ("outer", "core"))
    sums = jnp.sum(pieces[:, count : count + 2 * depth].astype(f32), axis=0)
    sums = sums[:depth] + sums[depth:]

    term = call(term_kernel, jax.ShapeDtypeStruct((half, block), bf16), window_all, pieces)
    sums = split_sum(sums, 0)
    sums = jnp.broadcast_to(sums[None], (nz * ny,) + sums.shape)
    pieces = exchange(jnp.concatenate([term.reshape(nz * ny, shard, block), sums], axis=1), ("z", "y"))

    pieces = call(
        functools.partial(sum_kernel, depth),
        jax.ShapeDtypeStruct((group, shard + 2 * depth, block), f32),
        pieces,
    )
    weight_grad, gain_grad, bias_grad = call(
        functools.partial(last_kernel, depth),
        (
            jax.ShapeDtypeStruct((shard, embed_width), f32),
            jax.ShapeDtypeStruct((window_width // block, block), f32),
            jax.ShapeDtypeStruct((window_width // block, block), f32),
        ),
        jnp.stack([outer, core]),
        exchange(pieces, ("outer", "core")),
        places=[smem, vmem],
    )
    gain_grad, bias_grad = gain_grad.reshape(window_width), bias_grad.reshape(window_width)

    scaled_grad = window_grad * ln_gain
    first_mean = jnp.sum(scaled_grad, axis=1, keepdims=True) / width
    second_mean = jnp.sum(scaled_grad * normed_head, axis=1, keepdims=True) / width
    grad_head = inv_std * (scaled_grad - first_mean - normed_head * second_mean)
    grad_tail = inv_std * (0.0 - first_mean - normed_tail * second_mean)
    feat_grad = jnp.concatenate([grad_head.astype(bf16), grad_tail.astype(bf16)], axis=1)
    return (feat_grad, weight_grad, gain_grad, bias_grad)


def solution(mesh):
    outer, dp = mesh.devices.shape
    fine = Mesh(mesh.devices.reshape(outer, 8, dp // 16, 2), ALL)
    in_specs = (
        P(ALL, None),
        P(),
        P(),
        P(DP, None),
        P(ALL, None),
        P(ALL),
        P(ALL),
        P("outer", None),
        P("outer", None),
        P("outer", None, None),
        P(ALL),
    )
    out_specs = (P(ALL, None), P(DP, None), P(), P())
    return jax.shard_map(body, mesh=fine, in_specs=in_specs, out_specs=out_specs, check_vma=False)
```

```python
import functools

import jax
import jax.numpy as jnp
from jax import lax
from jax.experimental import pallas as pl
from jax.experimental.pallas import tpu as pltpu
from jax.sharding import Mesh, PartitionSpec as P

logit_scale = 100.0
bf16 = jnp.bfloat16
f32 = jnp.float32
DP = ("z", "y", "core")
ALL = ("outer", "z", "y", "core")


def swap(value, axis, flip):
    size = lax.axis_size(axis)
    return lax.ppermute(value, axis, [(i, i ^ flip) for i in range(size)])


def split_sum(value, axis):
    high = lax.reduce_precision(value, 8, 7)
    return jnp.concatenate([high.astype(bf16), (value - high).astype(bf16)], axis=axis)


def exchange(pieces, axis):
    return lax.all_to_all(pieces, axis, split_axis=0, concat_axis=0, tiled=True)


def gather(value, axis):
    size = lax.axis_size(axis)
    return exchange(jnp.broadcast_to(value[None], (size,) + value.shape), axis)


def side_by_side(blocks):
    return jnp.concatenate([blocks[i] for i in range(blocks.shape[0])], axis=1)


def owner_tables(captions, owner_table, size_table, index_table, me):
    count = owner_table.shape[0]
    kmax = index_table.shape[1]
    held = 4
    mine = (owner_table == me).astype(jnp.int32)
    ids = jnp.arange(count, dtype=jnp.int32)
    before = jnp.sum(jnp.where(ids[None, :] < ids[:, None], mine[None, :], 0), axis=1)
    chosen = (mine[None, :] > 0) & (before[None, :] == jnp.arange(held, dtype=jnp.int32)[:, None])
    picked = jnp.sum(jnp.where(chosen, ids[None, :], 0), axis=1)
    lengths = jnp.sum(jnp.where(chosen, size_table[None, :], 0), axis=1)
    rows = index_table.at[picked].get(mode="promise_in_bounds")
    used = (jnp.arange(kmax, dtype=jnp.int32)[None, :] < lengths[:, None]).reshape(1, held * kmax)
    place = rows.reshape(held * kmax, 1) == jnp.arange(captions.shape[0], dtype=jnp.int32)[None, :]
    ordered = jnp.dot(place.astype(bf16), captions, preferred_element_type=f32).astype(bf16)
    return ordered, used


vmem = pl.BlockSpec(memory_space=pltpu.VMEM)
smem = pl.BlockSpec(memory_space=pltpu.SMEM)


def call(kernel, out_shape, *operands, places=None, scratch=()):
    return pl.pallas_call(
        kernel,
        out_shape=out_shape,
        in_specs=places or [vmem] * len(operands),
        scratch_shapes=scratch,
        compiler_params=pltpu.CompilerParams(vmem_limit_bytes=12 * 2**20),
    )(*operands)


def owner_kernel(kmax, parts, rows_ref, ordered_ref, used_ref, out_ref, lines):
    count, (held, width) = rows_ref.shape[0], ordered_ref.shape
    block = width // parts
    ordered = ordered_ref[...]
    labels = rows_ref[:, width:].astype(f32).astype(jnp.int32)
    local, target = labels[:, 0:1], labels[:, 1:2]
    columns = lax.broadcasted_iota(jnp.int32, (count, held), 1)
    first = local * kmax
    valid = (used_ref[...] > 0) & (columns >= first) & (columns < first + kmax)
    scores = logit_scale * lax.dot_general(
        rows_ref[:, :width], ordered, (((1,), (1,)), ((), ())), preferred_element_type=f32
    )
    highest = jnp.max(jnp.where(valid, scores, -jnp.inf), axis=1, keepdims=True)
    weights = jnp.where(valid, jnp.exp(scores - highest), 0.0)
    probs = weights / jnp.sum(weights, axis=1, keepdims=True)
    positive = jnp.where(columns == first + target, 1.0, 0.0)
    coefficients = (logit_scale * (probs - positive)).astype(bf16)
    gradient = jnp.dot(coefficients, ordered, preferred_element_type=f32)
    for i in range(parts):
        lines[pl.ds(i, count, stride=parts), :] = gradient[:, i * block : (i + 1) * block]
    out_ref[...] = lines[...].astype(bf16)


def sum_kernel(depth, pieces_ref, out_ref):
    size = out_ref.shape[1]
    total = pieces_ref[0].astype(f32)
    for i in range(1, pieces_ref.shape[0]):
        total += pieces_ref[i].astype(f32)
    tail = total[size - 2 * depth :]
    tail = tail + pltpu.roll(tail, depth, 0)
    for i in range(out_ref.shape[0]):
        out_ref[i, : size - 2 * depth, :] = total[: size - 2 * depth]
        out_ref[i, size - 2 * depth :, :] = tail


def last_kernel(depth, at_ref, last_ref, weight_ref, gain_ref, bias_ref):
    group, _, block = last_ref.shape
    shard, width = weight_ref.shape
    cores = group * block // width
    for i in range(width // block):
        weight_ref[:, i * block : (i + 1) * block] = last_ref[i * cores + at_ref[1], :shard, :]
    for i in range(group // 2):
        gain_ref[i * depth : (i + 1) * depth, :] = last_ref[i, shard : shard + depth, :]
        bias_ref[i * depth : (i + 1) * depth, :] = last_ref[i + group // 2, shard : shard + depth, :]


def owner_kernel(kmax, parts, rows_ref, ordered_ref, used_ref, out_ref, lines):
    count, (held, width) = rows_ref.shape[0], ordered_ref.shape
    block = width // parts
    ordered = ordered_ref[...]
    labels = rows_ref[:, width:].astype(f32).astype(jnp.int32)
    local, target = labels[:, 0:1], labels[:, 1:2]
    columns = lax.broadcasted_iota(jnp.int32, (count, held), 1)
    first = local * kmax
    valid = (used_ref[...] > 0) & (columns >= first) & (columns < first + kmax)
    scores = logit_scale * lax.dot_general(
        rows_ref[:, :width], ordered, (((1,), (1,)), ((), ())), preferred_element_type=f32
    )
    highest = jnp.max(jnp.where(valid, scores, -jnp.inf), axis=1, keepdims=True)
    weights = jnp.where(valid, jnp.exp(scores - highest), 0.0)
    probs = weights / jnp.sum(weights, axis=1, keepdims=True)
    positive = jnp.where(columns == first + target, 1.0, 0.0)
    coefficients = (logit_scale * (probs - positive)).astype(bf16)
    gradient = jnp.dot(coefficients, ordered, preferred_element_type=f32).astype(bf16)
    size = 16 * parts
    row = lax.broadcasted_iota(jnp.int32, (size, size), 0)
    column = lax.broadcasted_iota(jnp.int32, (size, size), 1)
    order = jnp.where(column == lax.rem(row, parts) * 16 + lax.div(row, parts), 1.0, 0.0).astype(bf16)
    for at in range(0, count, 16):
        some = jnp.concatenate([gradient[at : at + 16, i * block : (i + 1) * block] for i in range(parts)], axis=0)
        out_ref[at * parts : (at + 16) * parts, :] = jnp.dot(order, some, preferred_element_type=f32).astype(bf16)


def gradient_kernel(
    parts, depth, back_ref, slots_ref, unit_ref, norm_ref, cot_ref, weight_ref, normed_ref, pieces_ref, grad_ref
):
    group, rows, block = pieces_ref.shape
    count = unit_ref.shape[0]
    back, unit, slots = back_ref[...], unit_ref[...], slots_ref[...]
    columns = lax.broadcasted_iota(jnp.int32, (count, back.shape[0]), 1)
    blocks = []
    for i in range(parts):
        here = jnp.where(columns == slots * parts + i, 1.0, 0.0).astype(bf16)
        blocks.append(jnp.dot(here, back, preferred_element_type=f32))
    unit_grad = cot_ref[...] * jnp.concatenate(blocks, axis=1)
    along = jnp.sum(unit * unit_grad, axis=1, keepdims=True)
    proj = ((unit_grad - unit * along) / norm_ref[...]).astype(bf16)
    window_grad = lax.dot_general(
        proj, weight_ref[...], (((1,), (1,)), ((), ())), preferred_element_type=f32
    )
    grad_ref[...] = window_grad
    gain = jnp.sum(window_grad * normed_ref[...], axis=0, keepdims=True)
    bias = jnp.sum(window_grad, axis=0, keepdims=True)
    place = lax.broadcasted_iota(jnp.int32, (rows - count, block), 0)
    for g in range(group):
        tail = jnp.zeros((rows - count, block), f32)
        values, at = (gain, g) if g < group // 2 else (bias, g - group // 2)
        for r in range(depth):
            line = values[:, (at * depth + r) * block : (at * depth + r + 1) * block]
            high = line.astype(bf16).astype(f32)
            tail = jnp.where(place == r, high, jnp.where(place == depth + r, line - high, tail))
        i = g * parts // group
        pieces_ref[g, :count, :] = proj[:, i * block : (i + 1) * block]
        pieces_ref[g, count:, :] = tail.astype(bf16)


def term_kernel(windows_ref, pieces_ref, out_ref):
    groups, height, width = windows_ref.shape
    count = width // 2
    step = height // 4
    proj = [
        jnp.concatenate([pieces_ref[2 * g, :count, :], pieces_ref[2 * g + 1, :count, :]], axis=0)
        for g in range(groups)
    ]
    for at in range(0, height, step):
        total = jnp.dot(windows_ref[0, at : at + step, :], proj[0], preferred_element_type=f32)
        for g in range(1, groups):
            total += jnp.dot(windows_ref[g, at : at + step, :], proj[g], preferred_element_type=f32)
        out_ref[at : at + step, :] = total.astype(bf16)


def body(
    feats,
    ln_gain,
    ln_bias,
    head_weight,
    captions,
    image_cluster,
    image_target,
    cluster_owner,
    cluster_size,
    cap_index,
    cotangent,
):
    count, width = feats.shape
    window_width = ln_gain.shape[0]
    embed_width = head_weight.shape[1]
    shard = head_weight.shape[0]
    nz, ny, nc = lax.axis_size("z"), lax.axis_size("y"), lax.axis_size("core")
    dp_count = nz * ny * nc
    half = window_width // nc
    core = lax.axis_index("core")
    me = lax.axis_index(DP)
    capacity = 2
    kmax = cap_index.shape[2]
    owner_table = cluster_owner[0]

    outer = lax.axis_index("outer")
    n_outer = lax.axis_size("outer")
    block = embed_width // n_outer
    columns = lax.dynamic_slice_in_dim(head_weight, outer * block, block, 1)
    columns = gather(columns, ("z", "y")).reshape(half, block)
    blocks = gather(columns, "outer")

    widened = feats.astype(f32)
    means = jnp.mean(widened, axis=1, keepdims=True)
    centred = widened - means
    inv_std = lax.rsqrt(jnp.mean(centred * centred, axis=1, keepdims=True) + 1e-05)
    normed_head = centred[:, :window_width] * inv_std
    normed_tail = centred[:, window_width:] * inv_std
    window_bf = (normed_head * ln_gain + ln_bias).astype(bf16)
    by_feature = window_bf.T.reshape(nz * ny, nc, shard, count)
    window_own = lax.dynamic_index_in_dim(by_feature, core, 1, keepdims=False).reshape(half, count)
    window_other = lax.dynamic_index_in_dim(by_feature, 1 - core, 1, keepdims=False).reshape(half, count)
    window_sent = swap(window_other, "core", 1)
    window_pair = jnp.concatenate(
        [jnp.where(core == 0, window_own, window_sent), jnp.where(core == 0, window_sent, window_own)], axis=1
    )

    ids = jnp.arange(owner_table.shape[0], dtype=jnp.int32)[None, :]
    owners = jnp.sum(jnp.where(image_cluster[:, None] == ids, owner_table[None, :], 0), axis=1)
    local = jnp.sum(
        ((owner_table[None, :] == owners[:, None]) & (ids < image_cluster[:, None])).astype(jnp.int32), axis=1
    )
    images = jnp.arange(count, dtype=jnp.int32)
    ranks = jnp.sum(
        ((owners[:, None] == owners[None, :]) & (images[None, :] < images[:, None])).astype(jnp.int32), axis=1
    )
    slots = owners * capacity + ranks
    labels = jnp.stack([local, image_target], axis=1).astype(bf16)
    labels = jnp.concatenate([labels, jnp.zeros((count, 126), bf16)], axis=1)
    ordered, used = owner_tables(captions, owner_table, cluster_size[0], cap_index[0], me)

    def by_rows(left, right):
        return lax.dot_general(left, right, (((0,), (0,)), ((), ())), preferred_element_type=f32)

    blocks, window_pair, slots, labels = lax.optimization_barrier((blocks, window_pair, slots, labels))
    place = (jnp.arange(dp_count * capacity, dtype=jnp.int32)[:, None] == slots[None, :]).astype(bf16)

    partial = by_rows(window_pair, side_by_side(blocks)).reshape(nc, count, embed_width)
    partial_own = lax.dynamic_index_in_dim(partial, core, 0, keepdims=False)
    partial_other = lax.dynamic_index_in_dim(partial, 1 - core, 0, keepdims=False)
    partial_sent = swap(partial_other, "core", 1)
    projected = partial_own + partial_sent
    blocks, window_pair, projected = lax.optimization_barrier((blocks, window_pair, projected))
    weight_all = lax.all_gather(blocks, "core", axis=0)
    window_all = lax.all_gather(window_pair, "outer", axis=0)
    norm_len = jnp.sqrt(jnp.sum(projected * projected, axis=1, keepdims=True) + 1e-06)
    unit = projected / norm_len
    payload = jnp.concatenate([unit.astype(bf16), labels], axis=1)
    send_rows = jnp.dot(place, payload, preferred_element_type=f32).astype(bf16)
    received = lax.all_to_all(
        send_rows.reshape(dp_count, capacity, -1), DP, split_axis=0, concat_axis=0, tiled=True
    )
    gradient = call(
        functools.partial(owner_kernel, kmax, n_outer),
        jax.ShapeDtypeStruct((dp_count * capacity * n_outer, block), bf16),
        received.reshape(dp_count * capacity, -1),
        ordered,
        used.astype(f32),
        scratch=[pltpu.VMEM((dp_count * capacity * n_outer, block), f32)],
    )
    weight_all = [side_by_side(weight_all[i]).reshape(nz * ny, 1, shard, embed_width) for i in range(nc)]
    full_weight = jnp.concatenate(weight_all, axis=1).reshape(window_width, embed_width)
    returned = exchange(gradient.reshape(dp_count, capacity * n_outer, block), DP).reshape(-1, block)

    group = n_outer * nc
    depth = 2 * window_width // (group * block)
    pieces, window_grad = call(
        functools.partial(gradient_kernel, n_outer, depth),
        (
            jax.ShapeDtypeStruct((group, count + 16, block), bf16),
            jax.ShapeDtypeStruct((count, window_width), f32),
        ),
        returned,
        slots[:, None],
        unit,
        norm_len,
        cotangent[:, None],
        full_weight,
        normed_head,
    )
    pieces = exchange(pieces, ("outer", "core"))
    sums = jnp.sum(pieces[:, count : count + 2 * depth].astype(f32), axis=0)
    sums = sums[:depth] + sums[depth:]

    term = call(term_kernel, jax.ShapeDtypeStruct((half, block), bf16), window_all, pieces)
    sums = split_sum(sums, 0)
    sums = jnp.broadcast_to(sums[None], (nz * ny,) + sums.shape)
    pieces = exchange(jnp.concatenate([term.reshape(nz * ny, shard, block), sums], axis=1), ("z", "y"))

    pieces = call(
        functools.partial(sum_kernel, depth),
        jax.ShapeDtypeStruct((group, shard + 2 * depth, block), f32),
        pieces,
    )
    weight_grad, gain_grad, bias_grad = call(
        functools.partial(last_kernel, depth),
        (
            jax.ShapeDtypeStruct((shard, embed_width), f32),
            jax.ShapeDtypeStruct((window_width // block, block), f32),
            jax.ShapeDtypeStruct((window_width // block, block), f32),
        ),
        jnp.stack([outer, core]),
        exchange(pieces, ("outer", "core")),
        places=[smem, vmem],
    )
    gain_grad, bias_grad = gain_grad.reshape(window_width), bias_grad.reshape(window_width)

    scaled_grad = window_grad * ln_gain
    first_mean = jnp.sum(scaled_grad, axis=1, keepdims=True) / width
    second_mean = jnp.sum(scaled_grad * normed_head, axis=1, keepdims=True) / width
    grad_head = inv_std * (scaled_grad - first_mean - normed_head * second_mean)
    grad_tail = inv_std * (0.0 - first_mean - normed_tail * second_mean)
    feat_grad = jnp.concatenate([grad_head.astype(bf16), grad_tail.astype(bf16)], axis=1)
    return (feat_grad, weight_grad, gain_grad, bias_grad)


def solution(mesh):
    outer, dp = mesh.devices.shape
    fine = Mesh(mesh.devices.reshape(outer, 8, dp // 16, 2), ALL)
    in_specs = (
        P(ALL, None),
        P(),
        P(),
        P(DP, None),
        P(ALL, None),
        P(ALL),
        P(ALL),
        P("outer", None),
        P("outer", None),
        P("outer", None, None),
        P(ALL),
    )
    out_specs = (P(ALL, None), P(DP, None), P(), P())
    return jax.shard_map(body, mesh=fine, in_specs=in_specs, out_specs=out_specs, check_vma=False)
```

```python
import functools

import jax
import jax.numpy as jnp
from jax import lax
from jax.experimental import pallas as pl
from jax.experimental.pallas import tpu as pltpu
from jax.sharding import Mesh, PartitionSpec as P

logit_scale = 100.0
bf16 = jnp.bfloat16
f32 = jnp.float32
DP = ("z", "y", "core")
ALL = ("outer", "z", "y", "core")


def swap(value, axis, flip):
    size = lax.axis_size(axis)
    return lax.ppermute(value, axis, [(i, i ^ flip) for i in range(size)])


def split_sum(value, axis):
    high = lax.reduce_precision(value, 8, 7)
    return jnp.concatenate([high.astype(bf16), (value - high).astype(bf16)], axis=axis)


def exchange(pieces, axis):
    return lax.all_to_all(pieces, axis, split_axis=0, concat_axis=0, tiled=True)


def gather(value, axis):
    size = lax.axis_size(axis)
    return exchange(jnp.broadcast_to(value[None], (size,) + value.shape), axis)


def side_by_side(blocks):
    return jnp.concatenate([blocks[i] for i in range(blocks.shape[0])], axis=1)


def owner_tables(captions, owner_table, size_table, index_table, me):
    count = owner_table.shape[0]
    kmax = index_table.shape[1]
    held = 4
    mine = (owner_table == me).astype(jnp.int32)
    ids = jnp.arange(count, dtype=jnp.int32)
    before = jnp.sum(jnp.where(ids[None, :] < ids[:, None], mine[None, :], 0), axis=1)
    chosen = (mine[None, :] > 0) & (before[None, :] == jnp.arange(held, dtype=jnp.int32)[:, None])
    picked = jnp.sum(jnp.where(chosen, ids[None, :], 0), axis=1)
    lengths = jnp.sum(jnp.where(chosen, size_table[None, :], 0), axis=1)
    rows = index_table.at[picked].get(mode="promise_in_bounds")
    used = (jnp.arange(kmax, dtype=jnp.int32)[None, :] < lengths[:, None]).reshape(1, held * kmax)
    place = rows.reshape(held * kmax, 1) == jnp.arange(captions.shape[0], dtype=jnp.int32)[None, :]
    ordered = jnp.dot(place.astype(bf16), captions, preferred_element_type=f32).astype(bf16)
    return ordered, used


vmem = pl.BlockSpec(memory_space=pltpu.VMEM)
smem = pl.BlockSpec(memory_space=pltpu.SMEM)


def call(kernel, out_shape, *operands, places=None, scratch=()):
    return pl.pallas_call(
        kernel,
        out_shape=out_shape,
        in_specs=places or [vmem] * len(operands),
        scratch_shapes=scratch,
        compiler_params=pltpu.CompilerParams(vmem_limit_bytes=12 * 2**20),
    )(*operands)


def owner_kernel(kmax, parts, rows_ref, ordered_ref, used_ref, out_ref, lines):
    count, (held, width) = rows_ref.shape[0], ordered_ref.shape
    block = width // parts
    ordered = ordered_ref[...]
    labels = rows_ref[:, width:].astype(f32).astype(jnp.int32)
    local, target = labels[:, 0:1], labels[:, 1:2]
    columns = lax.broadcasted_iota(jnp.int32, (count, held), 1)
    first = local * kmax
    valid = (used_ref[...] > 0) & (columns >= first) & (columns < first + kmax)
    scores = logit_scale * lax.dot_general(
        rows_ref[:, :width], ordered, (((1,), (1,)), ((), ())), preferred_element_type=f32
    )
    highest = jnp.max(jnp.where(valid, scores, -jnp.inf), axis=1, keepdims=True)
    weights = jnp.where(valid, jnp.exp(scores - highest), 0.0)
    probs = weights / jnp.sum(weights, axis=1, keepdims=True)
    positive = jnp.where(columns == first + target, 1.0, 0.0)
    coefficients = (logit_scale * (probs - positive)).astype(bf16)
    gradient = jnp.dot(coefficients, ordered, preferred_element_type=f32)
    for i in range(parts):
        lines[pl.ds(i, count, stride=parts), :] = gradient[:, i * block : (i + 1) * block]
    out_ref[...] = lines[...].astype(bf16)


def sum_kernel(depth, pieces_ref, out_ref):
    size = out_ref.shape[1]
    total = pieces_ref[0].astype(f32)
    for i in range(1, pieces_ref.shape[0]):
        total += pieces_ref[i].astype(f32)
    tail = total[size - 2 * depth :]
    tail = tail + pltpu.roll(tail, depth, 0)
    for i in range(out_ref.shape[0]):
        out_ref[i, : size - 2 * depth, :] = total[: size - 2 * depth]
        out_ref[i, size - 2 * depth :, :] = tail


def last_kernel(depth, at_ref, last_ref, weight_ref, gain_ref, bias_ref):
    group, _, block = last_ref.shape
    shard, width = weight_ref.shape
    cores = group * block // width
    for i in range(width // block):
        weight_ref[:, i * block : (i + 1) * block] = last_ref[i * cores + at_ref[1], :shard, :]
    for i in range(group // 2):
        gain_ref[i * depth : (i + 1) * depth, :] = last_ref[i, shard : shard + depth, :]
        bias_ref[i * depth : (i + 1) * depth, :] = last_ref[i + group // 2, shard : shard + depth, :]


def owner_kernel(kmax, parts, rows_ref, ordered_ref, used_ref, out_ref, lines):
    count, (held, width) = rows_ref.shape[0], ordered_ref.shape
    block = width // parts
    ordered = ordered_ref[...]
    labels = rows_ref[:, width:].astype(f32).astype(jnp.int32)
    local, target = labels[:, 0:1], labels[:, 1:2]
    columns = lax.broadcasted_iota(jnp.int32, (count, held), 1)
    first = local * kmax
    valid = (used_ref[...] > 0) & (columns >= first) & (columns < first + kmax)
    scores = logit_scale * lax.dot_general(
        rows_ref[:, :width], ordered, (((1,), (1,)), ((), ())), preferred_element_type=f32
    )
    highest = jnp.max(jnp.where(valid, scores, -jnp.inf), axis=1, keepdims=True)
    weights = jnp.where(valid, jnp.exp(scores - highest), 0.0)
    probs = weights / jnp.sum(weights, axis=1, keepdims=True)
    positive = jnp.where(columns == first + target, 1.0, 0.0)
    coefficients = (logit_scale * (probs - positive)).astype(bf16)
    gradient = jnp.dot(coefficients, ordered, preferred_element_type=f32).astype(bf16)
    size = 16 * parts
    row = lax.broadcasted_iota(jnp.int32, (size, size), 0)
    column = lax.broadcasted_iota(jnp.int32, (size, size), 1)
    order = jnp.where(column == lax.rem(row, parts) * 16 + lax.div(row, parts), 1.0, 0.0).astype(bf16)
    for at in range(0, count, 16):
        some = jnp.concatenate([gradient[at : at + 16, i * block : (i + 1) * block] for i in range(parts)], axis=0)
        out_ref[at * parts : (at + 16) * parts, :] = jnp.dot(order, some, preferred_element_type=f32).astype(bf16)


def gradient_kernel(
    parts, depth, back_ref, slots_ref, unit_ref, norm_ref, cot_ref, weight_ref, normed_ref, pieces_ref, grad_ref
):
    group, rows, block = pieces_ref.shape
    count = unit_ref.shape[0]
    back, unit, slots = back_ref[...], unit_ref[...], slots_ref[...]
    columns = lax.broadcasted_iota(jnp.int32, (count, back.shape[0]), 1)
    blocks = []
    for i in range(parts):
        here = jnp.where(columns == slots * parts + i, 1.0, 0.0).astype(bf16)
        blocks.append(jnp.dot(here, back, preferred_element_type=f32))
    unit_grad = cot_ref[...] * jnp.concatenate(blocks, axis=1)
    along = jnp.sum(unit * unit_grad, axis=1, keepdims=True)
    proj = ((unit_grad - unit * along) / norm_ref[...]).astype(bf16)
    window_grad = lax.dot_general(
        proj, weight_ref[...], (((1,), (1,)), ((), ())), preferred_element_type=f32
    )
    grad_ref[...] = window_grad
    gain = jnp.sum(window_grad * normed_ref[...], axis=0, keepdims=True)
    bias = jnp.sum(window_grad, axis=0, keepdims=True)
    place = lax.broadcasted_iota(jnp.int32, (rows - count, block), 0)
    for g in range(group):
        tail = jnp.zeros((rows - count, block), f32)
        values, at = (gain, g) if g < group // 2 else (bias, g - group // 2)
        for r in range(depth):
            line = values[:, (at * depth + r) * block : (at * depth + r + 1) * block]
            high = line.astype(bf16).astype(f32)
            tail = jnp.where(place == r, high, jnp.where(place == depth + r, line - high, tail))
        i = g * parts // group
        pieces_ref[g, :count, :] = proj[:, i * block : (i + 1) * block]
        pieces_ref[g, count:, :] = tail.astype(bf16)


def term_kernel(windows_ref, pieces_ref, out_ref):
    groups, height, width = windows_ref.shape
    count = width // 2
    step = height // 4
    proj = [
        jnp.concatenate([pieces_ref[2 * g, :count, :], pieces_ref[2 * g + 1, :count, :]], axis=0)
        for g in range(groups)
    ]
    for at in range(0, height, step):
        total = jnp.dot(windows_ref[0, at : at + step, :], proj[0], preferred_element_type=f32)
        for g in range(1, groups):
            total += jnp.dot(windows_ref[g, at : at + step, :], proj[g], preferred_element_type=f32)
        out_ref[at : at + step, :] = total.astype(bf16)


def body(
    feats,
    ln_gain,
    ln_bias,
    head_weight,
    captions,
    image_cluster,
    image_target,
    cluster_owner,
    cluster_size,
    cap_index,
    cotangent,
):
    count, width = feats.shape
    window_width = ln_gain.shape[0]
    embed_width = head_weight.shape[1]
    shard = head_weight.shape[0]
    nz, ny, nc = lax.axis_size("z"), lax.axis_size("y"), lax.axis_size("core")
    dp_count = nz * ny * nc
    half = window_width // nc
    core = lax.axis_index("core")
    me = lax.axis_index(DP)
    capacity = 2
    kmax = cap_index.shape[2]
    owner_table = cluster_owner[0]

    outer = lax.axis_index("outer")
    n_outer = lax.axis_size("outer")
    block = embed_width // n_outer
    columns = lax.dynamic_slice_in_dim(head_weight, outer * block, block, 1)
    columns = gather(columns, ("z", "y")).reshape(half, block)
    cut = half * 5 // 8
    upper = lax.all_gather(columns[cut:], "outer", axis=0)
    blocks = jnp.concatenate([gather(columns[:cut], "outer"), upper], axis=1)

    widened = feats.astype(f32)
    means = jnp.mean(widened, axis=1, keepdims=True)
    centred = widened - means
    inv_std = lax.rsqrt(jnp.mean(centred * centred, axis=1, keepdims=True) + 1e-05)
    normed_head = centred[:, :window_width] * inv_std
    normed_tail = centred[:, window_width:] * inv_std
    window_bf = (normed_head * ln_gain + ln_bias).astype(bf16)
    by_feature = window_bf.T.reshape(nz * ny, nc, shard, count)
    window_own = lax.dynamic_index_in_dim(by_feature, core, 1, keepdims=False).reshape(half, count)
    window_other = lax.dynamic_index_in_dim(by_feature, 1 - core, 1, keepdims=False).reshape(half, count)
    window_sent = swap(window_other, "core", 1)
    window_pair = jnp.concatenate(
        [jnp.where(core == 0, window_own, window_sent), jnp.where(core == 0, window_sent, window_own)], axis=1
    )

    ids = jnp.arange(owner_table.shape[0], dtype=jnp.int32)[None, :]
    owners = jnp.sum(jnp.where(image_cluster[:, None] == ids, owner_table[None, :], 0), axis=1)
    local = jnp.sum(
        ((owner_table[None, :] == owners[:, None]) & (ids < image_cluster[:, None])).astype(jnp.int32), axis=1
    )
    images = jnp.arange(count, dtype=jnp.int32)
    ranks = jnp.sum(
        ((owners[:, None] == owners[None, :]) & (images[None, :] < images[:, None])).astype(jnp.int32), axis=1
    )
    slots = owners * capacity + ranks
    labels = jnp.stack([local, image_target], axis=1).astype(bf16)
    labels = jnp.concatenate([labels, jnp.zeros((count, 126), bf16)], axis=1)
    ordered, used = owner_tables(captions, owner_table, cluster_size[0], cap_index[0], me)

    def by_rows(left, right):
        return lax.dot_general(left, right, (((0,), (0,)), ((), ())), preferred_element_type=f32)

    blocks, window_pair, slots, labels = lax.optimization_barrier((blocks, window_pair, slots, labels))
    place = (jnp.arange(dp_count * capacity, dtype=jnp.int32)[:, None] == slots[None, :]).astype(bf16)

    partial = by_rows(window_pair, side_by_side(blocks)).reshape(nc, count, embed_width)
    partial_own = lax.dynamic_index_in_dim(partial, core, 0, keepdims=False)
    partial_other = lax.dynamic_index_in_dim(partial, 1 - core, 0, keepdims=False)
    partial_sent = swap(partial_other, "core", 1)
    projected = partial_own + partial_sent
    blocks, window_pair, projected = lax.optimization_barrier((blocks, window_pair, projected))
    weight_all = lax.all_gather(blocks, "core", axis=0)
    window_all = lax.all_gather(window_pair, "outer", axis=0)
    norm_len = jnp.sqrt(jnp.sum(projected * projected, axis=1, keepdims=True) + 1e-06)
    unit = projected / norm_len
    payload = jnp.concatenate([unit.astype(bf16), labels], axis=1)
    send_rows = jnp.dot(place, payload, preferred_element_type=f32).astype(bf16)
    received = lax.all_to_all(
        send_rows.reshape(dp_count, capacity, -1), DP, split_axis=0, concat_axis=0, tiled=True
    )
    gradient = call(
        functools.partial(owner_kernel, kmax, n_outer),
        jax.ShapeDtypeStruct((dp_count * capacity * n_outer, block), bf16),
        received.reshape(dp_count * capacity, -1),
        ordered,
        used.astype(f32),
        scratch=[pltpu.VMEM((dp_count * capacity * n_outer, block), f32)],
    )
    weight_all = [side_by_side(weight_all[i]).reshape(nz * ny, 1, shard, embed_width) for i in range(nc)]
    full_weight = jnp.concatenate(weight_all, axis=1).reshape(window_width, embed_width)
    returned = exchange(gradient.reshape(dp_count, capacity * n_outer, block), DP).reshape(-1, block)

    group = n_outer * nc
    depth = 2 * window_width // (group * block)
    pieces, window_grad = call(
        functools.partial(gradient_kernel, n_outer, depth),
        (
            jax.ShapeDtypeStruct((group, count + 16, block), bf16),
            jax.ShapeDtypeStruct((count, window_width), f32),
        ),
        returned,
        slots[:, None],
        unit,
        norm_len,
        cotangent[:, None],
        full_weight,
        normed_head,
    )
    pieces = exchange(pieces, ("outer", "core"))
    sums = jnp.sum(pieces[:, count : count + 2 * depth].astype(f32), axis=0)
    sums = sums[:depth] + sums[depth:]

    term = call(term_kernel, jax.ShapeDtypeStruct((half, block), bf16), window_all, pieces)
    sums = split_sum(sums, 0)
    sums = jnp.broadcast_to(sums[None], (nz * ny,) + sums.shape)
    pieces = exchange(jnp.concatenate([term.reshape(nz * ny, shard, block), sums], axis=1), ("z", "y"))

    pieces = call(
        functools.partial(sum_kernel, depth),
        jax.ShapeDtypeStruct((group, shard + 2 * depth, block), f32),
        pieces,
    )
    weight_grad, gain_grad, bias_grad = call(
        functools.partial(last_kernel, depth),
        (
            jax.ShapeDtypeStruct((shard, embed_width), f32),
            jax.ShapeDtypeStruct((window_width // block, block), f32),
            jax.ShapeDtypeStruct((window_width // block, block), f32),
        ),
        jnp.stack([outer, core]),
        exchange(pieces, ("outer", "core")),
        places=[smem, vmem],
    )
    gain_grad, bias_grad = gain_grad.reshape(window_width), bias_grad.reshape(window_width)

    scaled_grad = window_grad * ln_gain
    first_mean = jnp.sum(scaled_grad, axis=1, keepdims=True) / width
    second_mean = jnp.sum(scaled_grad * normed_head, axis=1, keepdims=True) / width
    grad_head = inv_std * (scaled_grad - first_mean - normed_head * second_mean)
    grad_tail = inv_std * (0.0 - first_mean - normed_tail * second_mean)
    feat_grad = jnp.concatenate([grad_head.astype(bf16), grad_tail.astype(bf16)], axis=1)
    return (feat_grad, weight_grad, gain_grad, bias_grad)


def solution(mesh):
    outer, dp = mesh.devices.shape
    fine = Mesh(mesh.devices.reshape(outer, 8, dp // 16, 2), ALL)
    in_specs = (
        P(ALL, None),
        P(),
        P(),
        P(DP, None),
        P(ALL, None),
        P(ALL),
        P(ALL),
        P("outer", None),
        P("outer", None),
        P("outer", None, None),
        P(ALL),
    )
    out_specs = (P(ALL, None), P(DP, None), P(), P())
    return jax.shard_map(body, mesh=fine, in_specs=in_specs, out_specs=out_specs, check_vma=False)
```
